256 devices in a mesh: seq: 64 (over z, x, core), tp: 4 (over y).
Axes of the slice: x: 4, y: 4, z: 8, core: 2. Of those that a mesh axis runs over, the one named last changes fastest.
Arguments:
- query: bfloat16 [32768, 2048], P('seq', 'tp'), may hold values from -6 to 6
- keys: bfloat16 [32768, 2048], P('seq', 'tp'), may hold values from -6 to 6
- values: bfloat16 [32768, 2048], P('seq', 'tp'), may hold values from -7 to 7
- beta: float32 [16], P('tp'), may hold values from -2 to 2
- out_weight: bfloat16 [2048, 2048], P('tp'), may hold values from -0.125 to 0.125
- cotangent: bfloat16 [32768, 2048], P(('seq', 'tp')), may hold values from -6 to 6
Outputs:
- output: bfloat16 [32768, 2048], P(('seq', 'tp'))
- grad_query: bfloat16 [32768, 2048], P('seq', 'tp')
- grad_keys: bfloat16 [32768, 2048], P('seq', 'tp')
- grad_values: bfloat16 [32768, 2048], P('seq', 'tp')
The draws below stay inside these ranges and needn't reach their ends.
All inputs are finite; a program needn't handle non-finite values.
Results may differ from the reference program's by a relative error of at most 0.0055.
The reference program's roundings to bfloat16 on the way (of `probs_b`, `mixed`, `grad_mixed`, `grad_local` and `grad_scores`) count: a program that leaves them out, or rounds other values in their place, can miss the bound.
Values may be sent and summed in bfloat16 or wider, within the bound.
A program may use at most 128 MiB of HBM per device.

```python
import jax
import jax.numpy as jnp
from jax import lax

D = 2048
HEADS = 16
HD = 128
TOK_DEV = 512
TOKENS = 32768


def query_and_keys(key):
    width = HEADS * HD
    first = jax.random.fold_in(key, 11)
    second = jax.random.fold_in(key, 12)
    query_out = jnp.clip(jax.random.normal(first, (TOKENS, width), jnp.float32), -4.0, 4.0)
    keys_out = jnp.clip(jax.random.normal(second, (TOKENS, width), jnp.float32), -4.0, 4.0)
    return (query_out, keys_out)


def draw_query(key, part):
    return query_and_keys(key)[0].astype(jnp.bfloat16)


def draw_keys(key, part):
    return query_and_keys(key)[1].astype(jnp.bfloat16)


def draw_values(key, part):
    width = HEADS * HD
    segment_count = TOKENS // TOK_DEV
    first = jax.random.fold_in(key, 21)
    second = jax.random.fold_in(key, 22)
    noise = jnp.clip(jax.random.normal(first, (segment_count, TOK_DEV, width), jnp.float32), -4.0, 4.0)
    means = jnp.clip(jax.random.normal(second, (segment_count, 1, width), jnp.float32), -3.0, 3.0)
    return (noise + means).reshape(TOKENS, width).astype(jnp.bfloat16)


def block_scale(own_key, dims, shards, least, top_value):
    gain, own = 1.0, jax.random.fold_in(own_key, 6)
    for dim, blocks in shards:
        heights = jnp.exp(jax.random.uniform(jax.random.fold_in(own, dim), (blocks,), jnp.float32, least / len(shards), top_value / len(shards)))
        gain = gain * jnp.repeat(heights, dims[dim] // blocks).reshape([-1 if axis == dim else 1 for axis in range(len(dims))])
    return gain


def bell_draw(own_key, dims, scale, most, split=(), held_as=jnp.bfloat16):
    entries = jax.random.normal(own_key, dims, jnp.float32) * scale
    if len(split) > 0:
        entries = block_scale(own_key, dims, split, -0.22, 0.18) * entries
    return jnp.clip(entries, min=-most, max=most).astype(held_as)


def setup_inputs(seed: int = 0) -> dict:
    arg_keys = jax.random.split(jax.random.key(seed), 7)
    return {
        "query": draw_query(jax.random.fold_in(arg_keys[6], 71), 0),
        "keys": draw_keys(jax.random.fold_in(arg_keys[6], 71), 0),
        "values": draw_values(jax.random.fold_in(arg_keys[6], 71), 0),
        "beta": jnp.clip(jax.random.uniform(arg_keys[3], (HEADS,), jnp.float32, -2.0, 2.0) * block_scale(arg_keys[3], (HEADS,), ((0, 4),), -0.4, 0.0), -2.0, 2.0),
        "out_weight": bell_draw(arg_keys[4], (HEADS * HD, D), (HEADS * HD) ** -0.5, 0.125, ((0, 4),)),
        "cotangent": bell_draw(arg_keys[5], (TOKENS, D), 1.0, 6.0, ((0, 256),)),
    }


highest = lax.Precision.HIGHEST

def plus_one(inputs):
    return jnp.where(inputs > 0, inputs + 1.0, jnp.exp(jnp.minimum(inputs, 0.0)))

def slope_of(inputs):
    return jnp.where(inputs > 0, jnp.ones_like(inputs), jnp.exp(jnp.minimum(inputs, 0.0)))

def batched(form, left, right):
    return jnp.einsum(form, left.astype(jnp.float32), right.astype(jnp.float32), precision=highest, preferred_element_type=jnp.float32)

def local_memory(keys_seg, values_seg):
    key_feat = plus_one(keys_seg.astype(jnp.float32))
    return (batched('lhc,lhd->hcd', key_feat, values_seg), lax.optimization_barrier(jnp.sum(key_feat, 0)))

def attention_probs(query_seg, keys_seg):
    length = query_seg.shape[0]
    scores = batched('lhc,mhc->hlm', query_seg, keys_seg) * HD ** (-0.5)
    causal = jnp.arange(length)[:, None] >= jnp.arange(length)[None, :]
    scores = jnp.where(causal[None], scores, -jnp.inf)
    top_score = lax.optimization_barrier(jnp.max(scores, -1, keepdims=True))
    expo = jnp.exp(scores - top_score)
    return expo / lax.optimization_barrier(jnp.sum(expo, -1, keepdims=True))

def memory_read(query_seg, memory, memory_sum):
    query_feat = plus_one(query_seg.astype(jnp.float32))
    numer = batched('lhc,hcd->lhd', query_feat, memory)
    denom = batched('lhc,hc->lh', query_feat, memory_sum) + 1.0
    return (query_feat, numer / denom[..., None], denom)

def segment_forward(query_seg, keys_seg, values_seg, memory, memory_sum, gate_mix):
    probs_b = attention_probs(query_seg, keys_seg).astype(jnp.bfloat16)
    local_out = batched('hlm,mhc->lhc', probs_b, values_seg)
    query_feat, mem_out, denom = memory_read(query_seg, memory, memory_sum)
    mixed = gate_mix[None, :, None] * mem_out + (1.0 - gate_mix)[None, :, None] * local_out
    return mixed.astype(jnp.bfloat16)

def memory_grads(query_seg, memory, memory_sum, grad_b, gate_mix):
    query_feat, mem_out, denom = memory_read(query_seg, memory, memory_sum)
    grad_mem = gate_mix[None, :, None] * grad_b.astype(jnp.float32)
    grad_numer = grad_mem / denom[..., None]
    grad_denom = -lax.optimization_barrier(jnp.sum(grad_mem * mem_out, -1)) / denom
    return (query_feat, grad_numer, grad_denom)

def segment_memory_grad(query_seg, memory, memory_sum, grad_b, gate_mix):
    query_feat, grad_numer, grad_denom = memory_grads(query_seg, memory, memory_sum, grad_b, gate_mix)
    return (batched('lhc,lhd->hcd', query_feat, grad_numer), batched('lh,lhc->hc', grad_denom, query_feat))

def segment_backward(query_seg, keys_seg, values_seg, memory, memory_sum, later_memory, later_sum, grad_b, gate_mix):
    probs = attention_probs(query_seg, keys_seg)
    probs_b = probs.astype(jnp.bfloat16)
    grad_local = ((1.0 - gate_mix)[None, :, None] * grad_b.astype(jnp.float32)).astype(jnp.bfloat16)
    grad_probs = batched('lhc,mhc->hlm', grad_local, values_seg)
    delta = lax.optimization_barrier(jnp.sum(probs * grad_probs, -1, keepdims=True))
    grad_scores = (probs * (grad_probs - delta) * HD ** (-0.5)).astype(jnp.bfloat16)
    query_local = batched('hlm,mhc->lhc', grad_scores, keys_seg)
    keys_local = batched('hlm,lhc->mhc', grad_scores, query_seg)
    values_local = batched('hlm,lhc->mhc', probs_b, grad_local)
    query_feat, grad_numer, grad_denom = memory_grads(query_seg, memory, memory_sum, grad_b, gate_mix)
    grad_qfeat = batched('lhd,hcd->lhc', grad_numer, memory) + grad_denom[..., None] * memory_sum[None]
    key_feat = plus_one(keys_seg.astype(jnp.float32))
    grad_kfeat = batched('lhd,hcd->lhc', values_seg, later_memory) + later_sum[None]
    values_mem = batched('lhc,hcd->lhd', key_feat, later_memory)
    grad_query = (query_local + grad_qfeat * slope_of(query_seg.astype(jnp.float32))).astype(jnp.bfloat16)
    grad_keys = (keys_local + grad_kfeat * slope_of(keys_seg.astype(jnp.float32))).astype(jnp.bfloat16)
    grad_values = (values_local + values_mem).astype(jnp.bfloat16)
    return (grad_query, grad_keys, grad_values)

def reference(query, keys, values, beta, out_weight, cotangent):
    segment_count = TOKENS // TOK_DEV

    def shaped(tensor):
        return tensor.reshape(segment_count, TOK_DEV, HEADS, HD)
    query_s, keys_s, values_s = (shaped(query), shaped(keys), shaped(values))
    gate_mix = jax.nn.sigmoid(beta.astype(jnp.float32))
    own_memory, own_sum = lax.map(lambda block: local_memory(block[0], block[1]), (keys_s, values_s))
    memory = jnp.concatenate([jnp.zeros_like(own_memory[:1]), jnp.cumsum(own_memory, 0)[:-1]], 0)
    memory_sum = jnp.concatenate([jnp.zeros_like(own_sum[:1]), jnp.cumsum(own_sum, 0)[:-1]], 0)
    mixed = lax.map(lambda block: segment_forward(block[0], block[1], block[2], block[3], block[4], gate_mix), (query_s, keys_s, values_s, memory, memory_sum))
    flat = mixed.reshape(TOKENS, HEADS * HD)
    output = jnp.dot(flat, out_weight, preferred_element_type=jnp.float32).astype(jnp.bfloat16)
    grad_mixed = lax.dot_general(cotangent, out_weight, (((1,), (1,)), ((), ())), preferred_element_type=jnp.float32).astype(jnp.bfloat16)
    grad_s = shaped(grad_mixed)
    memory_grad, sum_grad = lax.map(lambda block: segment_memory_grad(block[0], block[1], block[2], block[3], gate_mix), (query_s, memory, memory_sum, grad_s))
    later_memory = jnp.concatenate([jnp.cumsum(memory_grad[::-1], 0)[::-1][1:], jnp.zeros_like(memory_grad[:1])], 0)
    later_sum = jnp.concatenate([jnp.cumsum(sum_grad[::-1], 0)[::-1][1:], jnp.zeros_like(sum_grad[:1])], 0)
    grad_query, grad_keys, grad_values = lax.map(lambda block: segment_backward(block[0], block[1], block[2], block[3], block[4], block[5], block[6], block[7], gate_mix), (query_s, keys_s, values_s, memory, memory_sum, later_memory, later_sum, grad_s))
    width = HEADS * HD
    return (output, grad_query.reshape(TOKENS, width), grad_keys.reshape(TOKENS, width), grad_values.reshape(TOKENS, width))
```

```python
import functools

import jax
import jax.numpy as jnp
from jax import lax
from jax.experimental import pallas as pl
from jax.experimental.pallas import tpu as pltpu
from jax.sharding import Mesh
from jax.sharding import PartitionSpec as P

HD = 128
SEQ = ("seq_0", "seq_1", "seq_2")
SEQ_TP = ("seq_0", "seq_1", "seq_2", "tp")
MESH = pl.DeviceIdType.MESH
F32 = jnp.float32
BF16 = jnp.bfloat16
BLOCK = 256
PAD = 16


def feat(x):
    return jnp.where(x > 0, x + 1.0, jnp.exp(jnp.minimum(x, 0.0)))


def slope(x):
    return jnp.where(x > 0, jnp.ones_like(x), jnp.exp(jnp.minimum(x, 0.0)))


def dot_nn(a, b):
    return jnp.dot(a, b, preferred_element_type=F32)


def dot_nt(a, b):
    return lax.dot_general(a, b, (((1,), (1,)), ((), ())), preferred_element_type=F32)


def dot_tn(a, b):
    return lax.dot_general(a, b, (((0,), (0,)), ((), ())), preferred_element_type=F32)


def kernel(
    zs, xs, cs, ts,
    q_in, k_in, v_in, beta, w_in, cot_in,
    out_o, gq_o, gk_o, gv_o,
    q_v, k_v, v_v, w_v, cot_v, load_sem,
    cot_send, cot_recv,
    parcel, got1, part, total, base, got2, back, got3,
    scan_send, scan_recv,
    probs, local_out, mem_out, rdenom, mixed, gm, kl, vl,
    pf, rs_src, rs_dst, rs_send, rs_recv,
    out_v, gq_v, gk_v, gv_v, store_sem,
):
    length, width = q_v.shape
    heads = width // HD
    rows = cot_in.shape[0]
    half = rows // 2
    group = xs * cs
    prow = parcel.shape[2] - PAD
    scale = HD ** (-0.5)

    z = lax.axis_index("seq_0")
    x = lax.axis_index("seq_1")
    c = lax.axis_index("seq_2")
    y = lax.axis_index("tp")
    g = x * cs + c
    right = lax.rem(y + 1, ts)
    left = lax.rem(y + ts - 1, ts)
    far = lax.rem(y + 2, ts)

    def at(x_=None, c_=None, z_=None, y_=None):
        return (
            z if z_ is None else z_,
            x if x_ is None else x_,
            c if c_ is None else c_,
            y if y_ is None else y_,
        )

    def member(p):
        return at(x_=p // cs, c_=lax.rem(p, cs))

    loads = []
    for i, (src, dst) in enumerate(
        ((k_in, k_v), (v_in, v_v), (q_in, q_v), (w_in, w_v), (cot_in, cot_v.at[y]))
    ):
        copy = pltpu.make_async_copy(src, dst, load_sem.at[i])
        copy.start()
        loads.append(copy)

    barrier = pltpu.get_barrier_semaphore()
    peers = [at(y_=left), at(y_=right)]
    peers += [member(lax.rem(g + d, group)) for d in range(1, group)]
    peers += [at(z_=lax.rem(z + d, zs)) for d in range(1, zs)]
    for peer in peers:
        pl.semaphore_signal(barrier, inc=1, device_id=peer, device_id_type=MESH)
    pl.semaphore_wait(barrier, len(peers))

    def remote(src, dst, send, recv, device):
        return pltpu.make_async_remote_copy(
            src_ref=src, dst_ref=dst, send_sem=send, recv_sem=recv,
            device_id=device, device_id_type=MESH,
        )

    first, second = pl.ds(0, half), pl.ds(half, half)

    def cot_copy(i, owner, part_, to, from_input):
        src = cot_in.at[part_] if from_input else cot_v.at[owner, part_]
        return remote(src, cot_v.at[owner, part_], cot_send.at[i], cot_recv.at[i], to)

    to_right, to_left = at(y_=right), at(y_=left)
    cot_out = [
        cot_copy(0, y, first, to_right, True),
        cot_copy(1, y, second, to_left, True),
        cot_copy(2, y, second, to_right, True),
        cot_copy(3, y, first, to_left, True),
        cot_copy(4, left, first, to_right, False),
        cot_copy(5, right, second, to_left, False),
    ]
    cot_arrive = [
        cot_copy(0, left, first, to_right, False),
        cot_copy(1, right, second, to_left, False),
        cot_copy(2, left, second, to_right, False),
        cot_copy(3, right, first, to_left, False),
        cot_copy(4, far, first, to_right, False),
        cot_copy(5, far, second, to_left, False),
    ]
    for i in range(4):
        cot_out[i].start()

    def cot_relay():
        for i in range(2):
            cot_arrive[i].wait_recv()
            cot_out[4 + i].start()

    def slices_out(s):
        return [
            remote(
                parcel.at[s, lax.rem(g + d, group)], got1.at[s, g],
                scan_send.at[s, 0, d], scan_recv.at[s, 0, d],
                member(lax.rem(g + d, group)),
            )
            for d in range(1, group)
        ]

    def slices_in(s):
        return [
            remote(
                parcel.at[s, g], got1.at[s, lax.rem(g + group - d, group)],
                scan_send.at[s, 0, d], scan_recv.at[s, 0, d],
                member(lax.rem(g + d, group)),
            )
            for d in range(1, group)
        ]

    def ahead(s, d):
        return z + d if s == 0 else z - d

    def behind(s, d):
        return z - d if s == 0 else z + d

    def inside(k):
        return jnp.logical_and(k >= 0, k < zs)

    def wrapped(k):
        return lax.rem(k + zs, zs)

    def total_out(s, d):
        return remote(
            total.at[s], got2.at[s, z], scan_send.at[s, 1, d], scan_recv.at[s, 1, d],
            at(z_=wrapped(ahead(s, d))),
        )

    def total_in(s, d):
        return remote(
            total.at[s], got2.at[s, wrapped(behind(s, d))],
            scan_send.at[s, 1, d], scan_recv.at[s, 1, d],
            at(z_=wrapped(ahead(s, d))),
        )

    def back_out(s):
        return [
            remote(
                back.at[s, lax.rem(g + d, group)], got3.at[s, g],
                scan_send.at[s, 2, d], scan_recv.at[s, 2, d],
                member(lax.rem(g + d, group)),
            )
            for d in range(1, group)
        ]

    def back_in(s):
        return [
            remote(
                back.at[s, g], got3.at[s, lax.rem(g + group - d, group)],
                scan_send.at[s, 2, d], scan_recv.at[s, 2, d],
                member(lax.rem(g + d, group)),
            )
            for d in range(1, group)
        ]

    def scan_put(s, h, memory, sums):
        wide = jnp.broadcast_to(sums, (PAD, HD)).astype(BF16)
        per = group // heads
        for j in range(per):
            parcel[s, h * per + j, 0:prow, :] = memory[j * prow : (j + 1) * prow].astype(BF16)
            parcel[s, h * per + j, prow : prow + PAD, :] = wide

    def scan_start(s):
        for copy in slices_out(s):
            copy.start()

    def scan_middle(s):
        got1[s, g] = parcel[s, g]
        for copy in slices_in(s):
            copy.wait_recv()
        run = jnp.zeros((prow + PAD, HD), F32)
        for p in range(group) if s == 0 else reversed(range(group)):
            part[p] = run
            run = run + got1[s, p].astype(F32)
        total[s] = run.astype(BF16)
        for d in range(1, zs):

            @pl.when(inside(ahead(s, d)))
            def _(d=d):
                total_out(s, d).start()

    def scan_back(s):
        base[...] = jnp.zeros_like(base)
        for d in range(1, zs):

            @pl.when(inside(behind(s, d)))
            def _(d=d):
                total_in(s, d).wait_recv()
                base[...] += got2[s, wrapped(behind(s, d))].astype(F32)

        for p in range(group):
            back[s, p] = (base[...] + part[p]).astype(BF16)
        got3[s, g] = back[s, g]
        for copy in back_out(s):
            copy.start()

    def scan_end(s):
        for copy in back_in(s):
            copy.wait_recv()

    def scan_get(s, h):
        per = group // heads
        memory = jnp.concatenate([got3[s, h * per + j, 0:prow, :] for j in range(per)], 0)
        sums = got3[s, h * per, prow : prow + PAD, :].astype(F32)[0:1]
        return memory, sums

    def scan_sent(s):
        for copy in slices_out(s):
            copy.wait_send()
        for d in range(1, zs):

            @pl.when(inside(ahead(s, d)))
            def _(d=d):
                total_out(s, d).wait_send()

        for copy in back_out(s):
            copy.wait_send()

    def cols(h):
        return pl.ds(h * HD, HD)

    def gate_of(h):
        return jax.nn.sigmoid(jnp.full((1, HD), beta[h], F32))

    blocks = length // BLOCK

    def attention(h):
        for i in range(blocks):
            q_rows, seen = pl.ds(i * BLOCK, BLOCK), pl.ds(0, (i + 1) * BLOCK)
            s_t = dot_nt(k_v[seen, cols(h)], q_v[q_rows, cols(h)]) * scale
            key_at = lax.broadcasted_iota(jnp.int32, s_t.shape, 0)
            query_at = lax.broadcasted_iota(jnp.int32, s_t.shape, 1) + i * BLOCK
            s_t = jnp.where(key_at <= query_at, s_t, -jnp.inf)
            e = jnp.exp(s_t - jnp.max(s_t, 0, keepdims=True))
            p = e * (1.0 / jnp.sum(e, 0, keepdims=True))
            probs[h, seen, q_rows] = p
            local_out[q_rows, cols(h)] = dot_tn(p.astype(BF16), v_v[seen, cols(h)])

    def attention_back(h):
        gate = gate_of(h)
        memory, sums = scan_get(0, h)
        for i in reversed(range(blocks)):
            q_rows, seen = pl.ds(i * BLOCK, BLOCK), pl.ds(0, (i + 1) * BLOCK)
            g_f = gm[q_rows, cols(h)].astype(F32)
            g_l = ((1.0 - gate) * g_f).astype(BF16)
            q_b = q_v[q_rows, cols(h)]
            p = probs[h, seen, q_rows]
            gp = dot_nt(v_v[seen, cols(h)], g_l)
            delta = jnp.sum(p * gp, 0, keepdims=True)
            gs = (p * (gp - delta) * scale).astype(BF16)
            k_add, v_add = dot_nn(gs, q_b), dot_nn(p.astype(BF16), g_l)
            if i == blocks - 1:
                kl[seen, cols(h)] = k_add
                vl[seen, cols(h)] = v_add
            else:
                kl[seen, cols(h)] += k_add
                vl[seen, cols(h)] += v_add
            g_m = gate * g_f
            rd = rdenom[h, q_rows, :]
            g_n = g_m * rd
            g_d = -jnp.sum(g_m * mem_out[q_rows, cols(h)], -1, keepdims=True) * rd
            g_q = dot_nt(g_n.astype(BF16), memory) + g_d * sums
            own = dot_tn(gs, k_v[seen, cols(h)])
            gq_v[q_rows, cols(h)] = (own + g_q * slope(q_b.astype(F32))).astype(BF16)

    loads[0].wait()
    loads[1].wait()
    for h in range(heads):
        kf = feat(k_v[:, cols(h)].astype(F32))
        scan_put(0, h, dot_tn(kf.astype(BF16), v_v[:, cols(h)]), jnp.sum(kf, 0, keepdims=True))
    scan_start(0)
    loads[2].wait()
    attention(0)
    scan_middle(0)
    attention(1)
    scan_back(0)
    cot_relay()
    for h in range(2, heads):
        attention(h)
    scan_end(0)

    for h in range(heads):
        gate = gate_of(h)
        memory, sums = scan_get(0, h)
        qf = feat(q_v[:, cols(h)].astype(F32))
        rd = 1.0 / (jnp.sum(qf * sums, -1, keepdims=True) + 1.0)
        rdenom[h] = rd
        m_o = dot_nn(qf.astype(BF16), memory) * rd
        mem_out[:, cols(h)] = m_o
        mixed[:, cols(h)] = (gate * m_o + (1.0 - gate) * local_out[:, cols(h)]).astype(BF16)

    loads[3].wait()
    loads[4].wait()

    def block_rows(b):
        return pl.ds(pl.multiple_of(b * rows, rows), rows)

    def project(b, slot):
        pf[slot] = dot_nn(mixed[block_rows(b), :], w_v[...])

    def rs_copy(i, to):
        return remote(rs_src.at[i], rs_dst.at[i], rs_send.at[i], rs_recv.at[i], to)

    rs = [rs_copy(i, to_right if i % 2 == 0 else to_left) for i in range(6)]

    def rs_start(i, piece):
        rs_src[i] = piece.astype(BF16)
        rs[i].start()

    project(far, 0)
    rs_start(0, pf[0, 0:half, :])
    rs_start(1, pf[0, half:rows, :])
    project(right, 1)
    rs_start(2, pf[1, half:rows, :])
    project(left, 2)
    rs_start(3, pf[2, 0:half, :])
    project(y, 3)

    def grad_in(b):
        gm[block_rows(b), :] = dot_nt(cot_v[b], w_v[...]).astype(BF16)

    grad_in(y)
    cot_arrive[2].wait_recv()
    grad_in(left)
    cot_arrive[3].wait_recv()
    grad_in(right)
    cot_arrive[4].wait_recv()
    cot_arrive[5].wait_recv()
    grad_in(far)

    for h in range(heads):
        qf = feat(q_v[:, cols(h)].astype(F32))
        g_m = gate_of(h) * gm[:, cols(h)].astype(F32)
        rd = rdenom[h]
        g_n = (g_m * rd).astype(BF16)
        g_d = -jnp.sum(g_m * mem_out[:, cols(h)], -1, keepdims=True) * rd
        scan_put(1, h, dot_tn(qf.astype(BF16), g_n), jnp.sum(g_d * qf, 0, keepdims=True))
    scan_start(1)
    attention_back(0)
    scan_middle(1)
    attention_back(1)
    scan_back(1)
    attention_back(2)
    rs[0].wait_recv()
    rs_start(4, pf[1, 0:half, :] + rs_dst[0].astype(F32))
    rs[1].wait_recv()
    rs_start(5, pf[2, half:rows, :] + rs_dst[1].astype(F32))
    attention_back(3)

    stores = [
        pltpu.make_async_copy(src, dst, store_sem.at[i])
        for i, (src, dst) in enumerate(
            ((gq_v, gq_o), (gk_v, gk_o), (gv_v, gv_o), (out_v, out_o))
        )
    ]
    stores[0].start()

    scan_end(1)
    for h in range(heads):
        memory, sums = scan_get(1, h)
        k_f = k_v[:, cols(h)].astype(F32)
        g_k = dot_nt(v_v[:, cols(h)], memory) + sums
        gk_v[:, cols(h)] = (kl[:, cols(h)] + g_k * slope(k_f)).astype(BF16)
        gv_v[:, cols(h)] = (vl[:, cols(h)] + dot_nn(feat(k_f).astype(BF16), memory)).astype(BF16)
    stores[1].start()
    stores[2].start()

    for i in range(2, 6):
        rs[i].wait_recv()
    out_v[0:half, :] = (
        pf[3, 0:half, :] + rs_dst[4].astype(F32) + rs_dst[3].astype(F32)
    ).astype(BF16)
    out_v[half:rows, :] = (
        pf[3, half:rows, :] + rs_dst[2].astype(F32) + rs_dst[5].astype(F32)
    ).astype(BF16)
    stores[3].start()

    for copy in cot_out:
        copy.wait_send()
    for copy in rs:
        copy.wait_send()
    scan_sent(0)
    scan_sent(1)
    for copy in stores:
        copy.wait()


def solution(mesh):
    split = Mesh(mesh.devices.reshape(8, 4, 2, mesh.shape["tp"]), SEQ_TP)
    zs, xs, cs, ts = split.devices.shape
    group = xs * cs

    def local(query, keys, values, beta, out_weight, cotangent):
        length, width = query.shape
        heads = width // HD
        rows, deep = cotangent.shape
        prow = heads * HD // group
        slab = prow + PAD
        vm = pltpu.VMEM
        dma = pltpu.SemaphoreType.DMA
        any_ = pl.BlockSpec(memory_space=pl.ANY)
        scratch = [
            vm((length, width), BF16), vm((length, width), BF16), vm((length, width), BF16),
            vm((width, deep), BF16), vm((ts, rows, deep), BF16), dma((5,)),
            dma((6,)), dma((6,)),
            vm((2, group, slab, HD), BF16), vm((2, group, slab, HD), BF16),
            vm((group, slab, HD), F32), vm((2, slab, HD), BF16), vm((slab, HD), F32),
            vm((2, zs, slab, HD), BF16),
            vm((2, group, slab, HD), BF16), vm((2, group, slab, HD), BF16),
            dma((2, 3, 8)), dma((2, 3, 8)),
            vm((heads, length, length), F32), vm((length, width), F32), vm((length, width), F32),
            vm((heads, length, 1), F32), vm((length, width), BF16), vm((length, width), BF16),
            vm((length, width), F32), vm((length, width), F32),
            vm((ts, rows, deep), F32), vm((6, rows // 2, deep), BF16), vm((6, rows // 2, deep), BF16),
            dma((6,)), dma((6,)),
            vm((rows, deep), BF16), vm((length, width), BF16), vm((length, width), BF16),
            vm((length, width), BF16), dma((4,)),
        ]
        return pl.pallas_call(
            functools.partial(kernel, zs, xs, cs, ts),
            out_shape=(
                jax.ShapeDtypeStruct((rows, deep), BF16),
                jax.ShapeDtypeStruct((length, width), BF16),
                jax.ShapeDtypeStruct((length, width), BF16),
                jax.ShapeDtypeStruct((length, width), BF16),
            ),
            in_specs=[any_, any_, any_, pl.BlockSpec(memory_space=pltpu.SMEM), any_, any_],
            out_specs=(any_, any_, any_, any_),
            scratch_shapes=scratch,
            compiler_params=pltpu.CompilerParams(
                collective_id=0, has_side_effects=True, vmem_limit_bytes=56 * 1024 * 1024
            ),
            cost_estimate=pl.CostEstimate(
                flops=5_000_000_000, bytes_accessed=8_000_000, transcendentals=2_000_000
            ),
            name="layer",
        )(query, keys, values, beta, out_weight, cotangent)

    placed = (P(SEQ, "tp"), P(SEQ, "tp"), P(SEQ, "tp"), P("tp"), P("tp", None), P(SEQ_TP, None))
    return jax.shard_map(
        local,
        mesh=split,
        in_specs=placed,
        out_specs=(P(SEQ_TP, None), P(SEQ, "tp"), P(SEQ, "tp"), P(SEQ, "tp")),
        check_vma=False,
    )
```

```python
import functools

import jax
import jax.numpy as jnp
from jax import lax
from jax.experimental import pallas as pl
from jax.experimental.pallas import tpu as pltpu
from jax.sharding import Mesh
from jax.sharding import PartitionSpec as P

HD = 128
SEQ = ("seq_0", "seq_1", "seq_2")
SEQ_TP = ("seq_0", "seq_1", "seq_2", "tp")
MESH = pl.DeviceIdType.MESH
F32 = jnp.float32
BF16 = jnp.bfloat16
BLOCK = 256
PAD = 16


def feat(x):
    return jnp.where(x > 0, x + 1.0, jnp.exp(jnp.minimum(x, 0.0)))


def slope(x):
    return jnp.where(x > 0, jnp.ones_like(x), jnp.exp(jnp.minimum(x, 0.0)))


def dot_nn(a, b):
    return jnp.dot(a, b, preferred_element_type=F32)


def dot_nt(a, b):
    return lax.dot_general(a, b, (((1,), (1,)), ((), ())), preferred_element_type=F32)


def dot_tn(a, b):
    return lax.dot_general(a, b, (((0,), (0,)), ((), ())), preferred_element_type=F32)


def kernel(
    zs, xs, cs, ts,
    q_in, k_in, v_in, beta, w_in, cot_in,
    out_v, gq_v, gk_v, gv_v,
    q_v, k_v, v_v, w_v, cot_v, load_sem,
    cot_send, cot_recv,
    parcel, got1, part, total, base, got2, back, got3,
    scan_send, scan_recv,
    probs, local_out, mem_out, rdenom, mixed, gm, kl, vl,
    pf, rs_src, rs_dst, rs_send, rs_recv,
):
    length, width = q_v.shape
    heads = width // HD
    rows = cot_in.shape[0]
    half = rows // 2
    group = xs * cs
    prow = parcel.shape[2] - PAD
    scale = HD ** (-0.5)

    z = lax.axis_index("seq_0")
    x = lax.axis_index("seq_1")
    c = lax.axis_index("seq_2")
    y = lax.axis_index("tp")
    g = x * cs + c
    right = lax.rem(y + 1, ts)
    left = lax.rem(y + ts - 1, ts)
    far = lax.rem(y + 2, ts)

    def at(x_=None, c_=None, z_=None, y_=None):
        return (
            z if z_ is None else z_,
            x if x_ is None else x_,
            c if c_ is None else c_,
            y if y_ is None else y_,
        )

    def member(p):
        return at(x_=p // cs, c_=lax.rem(p, cs))

    loads = []
    for i, (src, dst) in enumerate(
        ((k_in, k_v), (v_in, v_v), (q_in, q_v), (w_in, w_v), (cot_in, cot_v.at[y]))
    ):
        copy = pltpu.make_async_copy(src, dst, load_sem.at[i])
        copy.start()
        loads.append(copy)

    barrier = pltpu.get_barrier_semaphore()
    peers = [at(y_=left), at(y_=right)]
    peers += [member(lax.rem(g + d, group)) for d in range(1, group)]
    peers += [at(z_=lax.rem(z + d, zs)) for d in range(1, zs)]
    for peer in peers:
        pl.semaphore_signal(barrier, inc=1, device_id=peer, device_id_type=MESH)
    pl.semaphore_wait(barrier, len(peers))

    def remote(src, dst, send, recv, device):
        return pltpu.make_async_remote_copy(
            src_ref=src, dst_ref=dst, send_sem=send, recv_sem=recv,
            device_id=device, device_id_type=MESH,
        )

    first, second = pl.ds(0, half), pl.ds(half, half)

    def cot_copy(i, owner, part_, to, from_input):
        src = cot_in.at[part_] if from_input else cot_v.at[owner, part_]
        return remote(src, cot_v.at[owner, part_], cot_send.at[i], cot_recv.at[i], to)

    to_right, to_left = at(y_=right), at(y_=left)
    cot_out = [
        cot_copy(0, y, first, to_right, True),
        cot_copy(1, y, second, to_left, True),
        cot_copy(2, y, second, to_right, True),
        cot_copy(3, y, first, to_left, True),
        cot_copy(4, left, first, to_right, False),
        cot_copy(5, right, second, to_left, False),
    ]
    cot_arrive = [
        cot_copy(0, left, first, to_right, False),
        cot_copy(1, right, second, to_left, False),
        cot_copy(2, left, second, to_right, False),
        cot_copy(3, right, first, to_left, False),
        cot_copy(4, far, first, to_right, False),
        cot_copy(5, far, second, to_left, False),
    ]
    for i in range(4):
        cot_out[i].start()

    def cot_relay():
        for i in range(2):
            cot_arrive[i].wait_recv()
            cot_out[4 + i].start()

    def slices_out(s):
        return [
            remote(
                parcel.at[s, lax.rem(g + d, group)], got1.at[s, g],
                scan_send.at[s, 0, d], scan_recv.at[s, 0, d],
                member(lax.rem(g + d, group)),
            )
            for d in range(1, group)
        ]

    def slices_in(s):
        return [
            remote(
                parcel.at[s, g], got1.at[s, lax.rem(g + group - d, group)],
                scan_send.at[s, 0, d], scan_recv.at[s, 0, d],
                member(lax.rem(g + d, group)),
            )
            for d in range(1, group)
        ]

    def ahead(s, d):
        return z + d if s == 0 else z - d

    def behind(s, d):
        return z - d if s == 0 else z + d

    def inside(k):
        return jnp.logical_and(k >= 0, k < zs)

    def wrapped(k):
        return lax.rem(k + zs, zs)

    def total_out(s, d):
        return remote(
            total.at[s], got2.at[s, z], scan_send.at[s, 1, d], scan_recv.at[s, 1, d],
            at(z_=wrapped(ahead(s, d))),
        )

    def total_in(s, d):
        return remote(
            total.at[s], got2.at[s, wrapped(behind(s, d))],
            scan_send.at[s, 1, d], scan_recv.at[s, 1, d],
            at(z_=wrapped(ahead(s, d))),
        )

    def back_out(s):
        return [
            remote(
                back.at[s, lax.rem(g + d, group)], got3.at[s, g],
                scan_send.at[s, 2, d], scan_recv.at[s, 2, d],
                member(lax.rem(g + d, group)),
            )
            for d in range(1, group)
        ]

    def back_in(s):
        return [
            remote(
                back.at[s, g], got3.at[s, lax.rem(g + group - d, group)],
                scan_send.at[s, 2, d], scan_recv.at[s, 2, d],
                member(lax.rem(g + d, group)),
            )
            for d in range(1, group)
        ]

    def scan_put(s, h, memory, sums):
        wide = jnp.broadcast_to(sums, (PAD, HD)).astype(BF16)
        per = group // heads
        for j in range(per):
            parcel[s, h * per + j, 0:prow, :] = memory[j * prow : (j + 1) * prow].astype(BF16)
            parcel[s, h * per + j, prow : prow + PAD, :] = wide

    def scan_start(s):
        for copy in slices_out(s):
            copy.start()

    def scan_middle(s):
        got1[s, g] = parcel[s, g]
        for copy in slices_in(s):
            copy.wait_recv()
        run = jnp.zeros((prow + PAD, HD), F32)
        for p in range(group) if s == 0 else reversed(range(group)):
            part[p] = run
            run = run + got1[s, p].astype(F32)
        total[s] = run.astype(BF16)
        for d in range(1, zs):

            @pl.when(inside(ahead(s, d)))
            def _(d=d):
                total_out(s, d).start()

    def scan_back(s):
        base[...] = jnp.zeros_like(base)
        for d in range(1, zs):

            @pl.when(inside(behind(s, d)))
            def _(d=d):
                total_in(s, d).wait_recv()
                base[...] += got2[s, wrapped(behind(s, d))].astype(F32)

        for p in range(group):
            back[s, p] = (base[...] + part[p]).astype(BF16)
        got3[s, g] = back[s, g]
        for copy in back_out(s):
            copy.start()

    def scan_end(s):
        for copy in back_in(s):
            copy.wait_recv()

    def scan_get(s, h):
        per = group // heads
        memory = jnp.concatenate([got3[s, h * per + j, 0:prow, :] for j in range(per)], 0)
        sums = got3[s, h * per, prow : prow + PAD, :].astype(F32)[0:1]
        return memory, sums

    def scan_sent(s):
        for copy in slices_out(s):
            copy.wait_send()
        for d in range(1, zs):

            @pl.when(inside(ahead(s, d)))
            def _(d=d):
                total_out(s, d).wait_send()

        for copy in back_out(s):
            copy.wait_send()

    def cols(h):
        return pl.ds(h * HD, HD)

    def gate_of(h):
        return jax.nn.sigmoid(jnp.full((1, HD), beta[h], F32))

    blocks = length // BLOCK

    def attention(h):
        for i in range(blocks):
            q_rows, seen = pl.ds(i * BLOCK, BLOCK), pl.ds(0, (i + 1) * BLOCK)
            s_t = dot_nt(k_v[seen, cols(h)], q_v[q_rows, cols(h)]) * scale
            key_at = lax.broadcasted_iota(jnp.int32, s_t.shape, 0)
            query_at = lax.broadcasted_iota(jnp.int32, s_t.shape, 1) + i * BLOCK
            s_t = jnp.where(key_at <= query_at, s_t, -jnp.inf)
            e = jnp.exp(s_t - jnp.max(s_t, 0, keepdims=True))
            p = e * (1.0 / jnp.sum(e, 0, keepdims=True))
            probs[h, seen, q_rows] = p
            local_out[q_rows, cols(h)] = dot_tn(p.astype(BF16), v_v[seen, cols(h)])

    def attention_back(h):
        gate = gate_of(h)
        memory, sums = scan_get(0, h)
        for i in reversed(range(blocks)):
            q_rows, seen = pl.ds(i * BLOCK, BLOCK), pl.ds(0, (i + 1) * BLOCK)
            g_f = gm[q_rows, cols(h)].astype(F32)
            g_l = ((1.0 - gate) * g_f).astype(BF16)
            q_b = q_v[q_rows, cols(h)]
            p = probs[h, seen, q_rows]
            gp = dot_nt(v_v[seen, cols(h)], g_l)
            delta = jnp.sum(p * gp, 0, keepdims=True)
            gs = (p * (gp - delta) * scale).astype(BF16)
            k_add, v_add = dot_nn(gs, q_b), dot_nn(p.astype(BF16), g_l)
            if i == blocks - 1:
                kl[seen, cols(h)] = k_add
                vl[seen, cols(h)] = v_add
            else:
                kl[seen, cols(h)] += k_add
                vl[seen, cols(h)] += v_add
            g_m = gate * g_f
            rd = rdenom[h, q_rows, :]
            g_n = g_m * rd
            g_d = -jnp.sum(g_m * mem_out[q_rows, cols(h)], -1, keepdims=True) * rd
            g_q = dot_nt(g_n.astype(BF16), memory) + g_d * sums
            own = dot_tn(gs, k_v[seen, cols(h)])
            gq_v[q_rows, cols(h)] = (own + g_q * slope(q_b.astype(F32))).astype(BF16)

    loads[0].wait()
    loads[1].wait()
    for h in range(heads):
        kf = feat(k_v[:, cols(h)].astype(F32))
        scan_put(0, h, dot_tn(kf.astype(BF16), v_v[:, cols(h)]), jnp.sum(kf, 0, keepdims=True))
    scan_start(0)
    loads[2].wait()
    attention(0)
    scan_middle(0)
    attention(1)
    scan_back(0)
    cot_relay()
    for h in range(2, heads):
        attention(h)
    scan_end(0)

    for h in range(heads):
        gate = gate_of(h)
        memory, sums = scan_get(0, h)
        qf = feat(q_v[:, cols(h)].astype(F32))
        rd = 1.0 / (jnp.sum(qf * sums, -1, keepdims=True) + 1.0)
        rdenom[h] = rd
        m_o = dot_nn(qf.astype(BF16), memory) * rd
        mem_out[:, cols(h)] = m_o
        mixed[:, cols(h)] = (gate * m_o + (1.0 - gate) * local_out[:, cols(h)]).astype(BF16)

    loads[3].wait()
    loads[4].wait()

    def block_rows(b):
        return pl.ds(pl.multiple_of(b * rows, rows), rows)

    def project(b, slot):
        pf[slot] = dot_nn(mixed[block_rows(b), :], w_v[...])

    def rs_copy(i, to):
        return remote(rs_src.at[i], rs_dst.at[i], rs_send.at[i], rs_recv.at[i], to)

    rs = [rs_copy(i, to_right if i % 2 == 0 else to_left) for i in range(6)]

    def rs_start(i, piece):
        rs_src[i] = piece.astype(BF16)
        rs[i].start()

    project(far, 0)
    rs_start(0, pf[0, 0:half, :])
    rs_start(1, pf[0, half:rows, :])
    project(right, 1)
    rs_start(2, pf[1, half:rows, :])
    project(left, 2)
    rs_start(3, pf[2, 0:half, :])
    project(y, 3)

    def grad_in(b):
        gm[block_rows(b), :] = dot_nt(cot_v[b], w_v[...]).astype(BF16)

    grad_in(y)
    cot_arrive[2].wait_recv()
    grad_in(left)
    cot_arrive[3].wait_recv()
    grad_in(right)
    cot_arrive[4].wait_recv()
    cot_arrive[5].wait_recv()
    grad_in(far)

    for h in range(heads):
        qf = feat(q_v[:, cols(h)].astype(F32))
        g_m = gate_of(h) * gm[:, cols(h)].astype(F32)
        rd = rdenom[h]
        g_n = (g_m * rd).astype(BF16)
        g_d = -jnp.sum(g_m * mem_out[:, cols(h)], -1, keepdims=True) * rd
        scan_put(1, h, dot_tn(qf.astype(BF16), g_n), jnp.sum(g_d * qf, 0, keepdims=True))
    scan_start(1)
    attention_back(0)
    scan_middle(1)
    attention_back(1)
    scan_back(1)
    attention_back(2)
    rs[0].wait_recv()
    rs_start(4, pf[1, 0:half, :] + rs_dst[0].astype(F32))
    rs[1].wait_recv()
    rs_start(5, pf[2, half:rows, :] + rs_dst[1].astype(F32))
    attention_back(3)

    scan_end(1)
    for h in range(heads):
        memory, sums = scan_get(1, h)
        k_f = k_v[:, cols(h)].astype(F32)
        g_k = dot_nt(v_v[:, cols(h)], memory) + sums
        gk_v[:, cols(h)] = (kl[:, cols(h)] + g_k * slope(k_f)).astype(BF16)
        gv_v[:, cols(h)] = (vl[:, cols(h)] + dot_nn(feat(k_f).astype(BF16), memory)).astype(BF16)

    for i in range(2, 6):
        rs[i].wait_recv()
    out_v[0:half, :] = (
        pf[3, 0:half, :] + rs_dst[4].astype(F32) + rs_dst[3].astype(F32)
    ).astype(BF16)
    out_v[half:rows, :] = (
        pf[3, half:rows, :] + rs_dst[2].astype(F32) + rs_dst[5].astype(F32)
    ).astype(BF16)

    for copy in cot_out:
        copy.wait_send()
    for copy in rs:
        copy.wait_send()
    scan_sent(0)
    scan_sent(1)


def store(*refs):
    sources, targets, sem = refs[:4], refs[4:8], refs[8]
    copies = [
        pltpu.make_async_copy(src, dst, sem.at[i])
        for i, (src, dst) in enumerate(zip(sources, targets))
    ]
    for copy in copies:
        copy.start()
    for copy in copies:
        copy.wait()


def solution(mesh):
    split = Mesh(mesh.devices.reshape(8, 4, 2, mesh.shape["tp"]), SEQ_TP)
    zs, xs, cs, ts = split.devices.shape
    group = xs * cs

    def local(query, keys, values, beta, out_weight, cotangent):
        length, width = query.shape
        heads = width // HD
        rows, deep = cotangent.shape
        prow = heads * HD // group
        slab = prow + PAD
        vm = pltpu.VMEM
        dma = pltpu.SemaphoreType.DMA
        any_ = pl.BlockSpec(memory_space=pl.ANY)
        scratch = [
            vm((length, width), BF16), vm((length, width), BF16), vm((length, width), BF16),
            vm((width, deep), BF16), vm((ts, rows, deep), BF16), dma((5,)),
            dma((6,)), dma((6,)),
            vm((2, group, slab, HD), BF16), vm((2, group, slab, HD), BF16),
            vm((group, slab, HD), F32), vm((2, slab, HD), BF16), vm((slab, HD), F32),
            vm((2, zs, slab, HD), BF16),
            vm((2, group, slab, HD), BF16), vm((2, group, slab, HD), BF16),
            dma((2, 3, 8)), dma((2, 3, 8)),
            vm((heads, length, length), F32), vm((length, width), F32), vm((length, width), F32),
            vm((heads, length, 1), F32), vm((length, width), BF16), vm((length, width), BF16),
            vm((length, width), F32), vm((length, width), F32),
            vm((ts, rows, deep), F32), vm((6, rows // 2, deep), BF16), vm((6, rows // 2, deep), BF16),
            dma((6,)), dma((6,)),
        ]
        results = ((rows, deep), (length, width), (length, width), (length, width))
        held = pl.pallas_call(
            functools.partial(kernel, zs, xs, cs, ts),
            out_shape=tuple(vm(dims, BF16) for dims in results),
            in_specs=[any_, any_, any_, pl.BlockSpec(memory_space=pltpu.SMEM), any_, any_],
            out_specs=(pl.BlockSpec(memory_space=pltpu.VMEM),) * 4,
            scratch_shapes=scratch,
            compiler_params=pltpu.CompilerParams(
                collective_id=0, has_side_effects=True, vmem_limit_bytes=58 * 1024 * 1024
            ),
            cost_estimate=pl.CostEstimate(
                flops=5_000_000_000, bytes_accessed=8_000_000, transcendentals=2_000_000
            ),
            name="layer",
        )(query, keys, values, beta, out_weight, cotangent)
        return pl.pallas_call(
            store,
            out_shape=tuple(jax.ShapeDtypeStruct(dims, BF16) for dims in results),
            in_specs=[any_] * 4,
            out_specs=(any_,) * 4,
            scratch_shapes=[dma((4,))],
            compiler_params=pltpu.CompilerParams(vmem_limit_bytes=4 * 1024 * 1024),
            cost_estimate=pl.CostEstimate(flops=0, bytes_accessed=4_000_000, transcendentals=0),
            name="store",
        )(*held)

    placed = (P(SEQ, "tp"), P(SEQ, "tp"), P(SEQ, "tp"), P("tp"), P("tp", None), P(SEQ_TP, None))
    return jax.shard_map(
        local,
        mesh=split,
        in_specs=placed,
        out_specs=(P(SEQ_TP, None), P(SEQ, "tp"), P(SEQ, "tp"), P(SEQ, "tp")),
        check_vma=False,
    )
```

```python
import functools

import jax
import jax.numpy as jnp
from jax import lax
from jax.experimental import pallas as pl
from jax.experimental.pallas import tpu as pltpu
from jax.sharding import Mesh
from jax.sharding import PartitionSpec as P

HD = 128
SEQ = ("seq_0", "seq_1", "seq_2")
SEQ_TP = ("seq_0", "seq_1", "seq_2", "tp")
MESH = pl.DeviceIdType.MESH
F32 = jnp.float32
BF16 = jnp.bfloat16
BLOCK = 256
PAD = 16


def feat(x):
    return jnp.where(x > 0, x + 1.0, jnp.exp(jnp.minimum(x, 0.0)))


def slope(x):
    return jnp.where(x > 0, jnp.ones_like(x), jnp.exp(jnp.minimum(x, 0.0)))


def dot_nn(a, b):
    return jnp.dot(a, b, preferred_element_type=F32)


def dot_nt(a, b):
    return lax.dot_general(a, b, (((1,), (1,)), ((), ())), preferred_element_type=F32)


def dot_tn(a, b):
    return lax.dot_general(a, b, (((0,), (0,)), ((), ())), preferred_element_type=F32)


def kernel(
    zs, xs, cs, ts,
    q_in, k_in, v_in, beta, w_in, cot_in,
    out_v, gq_v, gk_v, gv_v,
    q_v, k_v, v_v, w_v, cot_v, load_sem,
    cot_send, cot_recv,
    parcel, got1, part, total, base, got2, back, got3,
    scan_send, scan_recv,
    probs, local_out, mem_out, rdenom, mixed, gm, kl, vl,
    pf, rs_src, rs_dst, rs_send, rs_recv,
):
    length, width = q_v.shape
    heads = width // HD
    rows = cot_in.shape[0]
    half = rows // 2
    group = xs * cs
    prow = parcel.shape[2] - PAD
    scale = HD ** (-0.5)

    z = lax.axis_index("seq_0")
    x = lax.axis_index("seq_1")
    c = lax.axis_index("seq_2")
    y = lax.axis_index("tp")
    g = x * cs + c
    right = lax.rem(y + 1, ts)
    left = lax.rem(y + ts - 1, ts)
    far = lax.rem(y + 2, ts)

    def at(x_=None, c_=None, z_=None, y_=None):
        return (
            z if z_ is None else z_,
            x if x_ is None else x_,
            c if c_ is None else c_,
            y if y_ is None else y_,
        )

    def member(p):
        return at(x_=p // cs, c_=lax.rem(p, cs))

    loads = []
    for i, (src, dst) in enumerate(
        ((k_in, k_v), (v_in, v_v), (q_in, q_v), (w_in, w_v), (cot_in, cot_v.at[y]))
    ):
        copy = pltpu.make_async_copy(src, dst, load_sem.at[i])
        copy.start()
        loads.append(copy)

    barrier = pltpu.get_barrier_semaphore()
    peers = [at(y_=left), at(y_=right)]
    peers += [member(lax.rem(g + d, group)) for d in range(1, group)]
    peers += [at(z_=lax.rem(z + d, zs)) for d in range(1, zs)]
    for peer in peers:
        pl.semaphore_signal(barrier, inc=1, device_id=peer, device_id_type=MESH)
    pl.semaphore_wait(barrier, len(peers))

    def remote(src, dst, send, recv, device):
        return pltpu.make_async_remote_copy(
            src_ref=src, dst_ref=dst, send_sem=send, recv_sem=recv,
            device_id=device, device_id_type=MESH,
        )

    first, second = pl.ds(0, half), pl.ds(half, half)

    def cot_copy(i, owner, part_, to, from_input):
        src = cot_in.at[part_] if from_input else cot_v.at[owner, part_]
        return remote(src, cot_v.at[owner, part_], cot_send.at[i], cot_recv.at[i], to)

    to_right, to_left = at(y_=right), at(y_=left)
    cot_out = [
        cot_copy(0, y, first, to_right, True),
        cot_copy(1, y, second, to_left, True),
        cot_copy(2, y, second, to_right, True),
        cot_copy(3, y, first, to_left, True),
        cot_copy(4, left, first, to_right, False),
        cot_copy(5, right, second, to_left, False),
    ]
    cot_arrive = [
        cot_copy(0, left, first, to_right, False),
        cot_copy(1, right, second, to_left, False),
        cot_copy(2, left, second, to_right, False),
        cot_copy(3, right, first, to_left, False),
        cot_copy(4, far, first, to_right, False),
        cot_copy(5, far, second, to_left, False),
    ]
    for i in range(4):
        cot_out[i].start()

    def cot_relay():
        for i in range(2):
            cot_arrive[i].wait_recv()
            cot_out[4 + i].start()

    def slices_out(s):
        return [
            remote(
                parcel.at[s, lax.rem(g + d, group)], got1.at[s, g],
                scan_send.at[s, 0, d], scan_recv.at[s, 0, d],
                member(lax.rem(g + d, group)),
            )
            for d in range(1, group)
        ]

    def slices_in(s):
        return [
            remote(
                parcel.at[s, g], got1.at[s, lax.rem(g + group - d, group)],
                scan_send.at[s, 0, d], scan_recv.at[s, 0, d],
                member(lax.rem(g + d, group)),
            )
            for d in range(1, group)
        ]

    def ahead(s, d):
        return z + d if s == 0 else z - d

    def behind(s, d):
        return z - d if s == 0 else z + d

    def inside(k):
        return jnp.logical_and(k >= 0, k < zs)

    def wrapped(k):
        return lax.rem(k + zs, zs)

    def total_out(s, d):
        return remote(
            total.at[s], got2.at[s, z], scan_send.at[s, 1, d], scan_recv.at[s, 1, d],
            at(z_=wrapped(ahead(s, d))),
        )

    def total_in(s, d):
        return remote(
            total.at[s], got2.at[s, wrapped(behind(s, d))],
            scan_send.at[s, 1, d], scan_recv.at[s, 1, d],
            at(z_=wrapped(ahead(s, d))),
        )

    def back_out(s):
        return [
            remote(
                back.at[s, lax.rem(g + d, group)], got3.at[s, g],
                scan_send.at[s, 2, d], scan_recv.at[s, 2, d],
                member(lax.rem(g + d, group)),
            )
            for d in range(1, group)
        ]

    def back_in(s):
        return [
            remote(
                back.at[s, g], got3.at[s, lax.rem(g + group - d, group)],
                scan_send.at[s, 2, d], scan_recv.at[s, 2, d],
                member(lax.rem(g + d, group)),
            )
            for d in range(1, group)
        ]

    def scan_put(s, h, memory, sums):
        wide = jnp.broadcast_to(sums, (PAD, HD)).astype(BF16)
        per = group // heads
        for j in range(per):
            parcel[s, h * per + j, 0:prow, :] = memory[j * prow : (j + 1) * prow].astype(BF16)
            parcel[s, h * per + j, prow : prow + PAD, :] = wide

    def scan_start(s):
        for copy in slices_out(s):
            copy.start()

    def scan_middle(s):
        got1[s, g] = parcel[s, g]
        for copy in slices_in(s):
            copy.wait_recv()
        run = jnp.zeros((prow + PAD, HD), F32)
        for p in range(group) if s == 0 else reversed(range(group)):
            part[p] = run
            run = run + got1[s, p].astype(F32)
        total[s] = run.astype(BF16)
        for d in range(1, zs):

            @pl.when(inside(ahead(s, d)))
            def _(d=d):
                total_out(s, d).start()

    def scan_back(s):
        base[...] = jnp.zeros_like(base)
        for d in range(1, zs):

            @pl.when(inside(behind(s, d)))
            def _(d=d):
                total_in(s, d).wait_recv()
                base[...] += got2[s, wrapped(behind(s, d))].astype(F32)

        for p in range(group):
            back[s, p] = (base[...] + part[p]).astype(BF16)
        got3[s, g] = back[s, g]
        for copy in back_out(s):
            copy.start()

    def scan_end(s):
        for copy in back_in(s):
            copy.wait_recv()

    def scan_get(s, h):
        per = group // heads
        memory = jnp.concatenate([got3[s, h * per + j, 0:prow, :] for j in range(per)], 0)
        sums = got3[s, h * per, prow : prow + PAD, :].astype(F32)[0:1]
        return memory, sums

    def scan_sent(s):
        for copy in slices_out(s):
            copy.wait_send()
        for d in range(1, zs):

            @pl.when(inside(ahead(s, d)))
            def _(d=d):
                total_out(s, d).wait_send()

        for copy in back_out(s):
            copy.wait_send()

    def cols(h):
        return pl.ds(h * HD, HD)

    def gate_of(h):
        return jax.nn.sigmoid(jnp.full((1, HD), beta[h], F32))

    blocks = length // BLOCK

    def attention(h):
        for i in range(blocks):
            q_rows, seen = pl.ds(i * BLOCK, BLOCK), pl.ds(0, (i + 1) * BLOCK)
            s_t = dot_nt(k_v[seen, cols(h)], q_v[q_rows, cols(h)]) * scale
            key_at = lax.broadcasted_iota(jnp.int32, s_t.shape, 0)
            query_at = lax.broadcasted_iota(jnp.int32, s_t.shape, 1) + i * BLOCK
            s_t = jnp.where(key_at <= query_at, s_t, -jnp.inf)
            e = jnp.exp(s_t - jnp.max(s_t, 0, keepdims=True))
            p = e * (1.0 / jnp.sum(e, 0, keepdims=True))
            probs[h, seen, q_rows] = p
            local_out[q_rows, cols(h)] = dot_tn(p.astype(BF16), v_v[seen, cols(h)])

    def attention_back(h):
        gate = gate_of(h)
        memory, sums = scan_get(0, h)
        for i in reversed(range(blocks)):
            q_rows, seen = pl.ds(i * BLOCK, BLOCK), pl.ds(0, (i + 1) * BLOCK)
            g_f = gm[q_rows, cols(h)].astype(F32)
            g_l = ((1.0 - gate) * g_f).astype(BF16)
            q_b = q_v[q_rows, cols(h)]
            p = probs[h, seen, q_rows]
            gp = dot_nt(v_v[seen, cols(h)], g_l)
            delta = jnp.sum(p * gp, 0, keepdims=True)
            gs = (p * (gp - delta) * scale).astype(BF16)
            k_add, v_add = dot_nn(gs, q_b), dot_nn(p.astype(BF16), g_l)
            if i == blocks - 1:
                kl[seen, cols(h)] = k_add
                vl[seen, cols(h)] = v_add
            else:
                kl[seen, cols(h)] += k_add
                vl[seen, cols(h)] += v_add
            g_m = gate * g_f
            rd = rdenom[h, q_rows, :]
            g_n = g_m * rd
            g_d = -jnp.sum(g_m * mem_out[q_rows, cols(h)], -1, keepdims=True) * rd
            g_q = dot_nt(g_n.astype(BF16), memory) + g_d * sums
            own = dot_tn(gs, k_v[seen, cols(h)])
            gq_v[q_rows, cols(h)] = (own + g_q * slope(q_b.astype(F32))).astype(BF16)

    loads[0].wait()
    loads[1].wait()
    for h in range(heads):
        kf = feat(k_v[:, cols(h)].astype(F32))
        scan_put(0, h, dot_tn(kf.astype(BF16), v_v[:, cols(h)]), jnp.sum(kf, 0, keepdims=True))
    scan_start(0)
    loads[2].wait()
    for h in range(heads):
        attention(h)
    scan_middle(0)
    cot_relay()

    def block_rows(b):
        return pl.ds(pl.multiple_of(b * rows, rows), rows)

    def grad_in(b):
        gm[block_rows(b), :] = dot_nt(cot_v[b], w_v[...]).astype(BF16)

    def project(b, slot):
        pf[slot] = dot_nn(mixed[block_rows(b), :], w_v[...])

    def rs_copy(i, to):
        return remote(rs_src.at[i], rs_dst.at[i], rs_send.at[i], rs_recv.at[i], to)

    rs = [rs_copy(i, to_right if i % 2 == 0 else to_left) for i in range(6)]

    def rs_start(i, piece):
        rs_src[i] = piece.astype(BF16)
        rs[i].start()

    loads[3].wait()
    loads[4].wait()
    grad_in(y)
    scan_back(0)
    cot_arrive[2].wait_recv()
    grad_in(left)
    cot_arrive[3].wait_recv()
    grad_in(right)
    scan_end(0)

    for h in range(heads):
        gate = gate_of(h)
        memory, sums = scan_get(0, h)
        qf = feat(q_v[:, cols(h)].astype(F32))
        rd = 1.0 / (jnp.sum(qf * sums, -1, keepdims=True) + 1.0)
        rdenom[h] = rd
        m_o = dot_nn(qf.astype(BF16), memory) * rd
        mem_out[:, cols(h)] = m_o
        mixed[:, cols(h)] = (gate * m_o + (1.0 - gate) * local_out[:, cols(h)]).astype(BF16)

    project(far, 0)
    rs_start(0, pf[0, 0:half, :])
    rs_start(1, pf[0, half:rows, :])
    cot_arrive[4].wait_recv()
    cot_arrive[5].wait_recv()
    grad_in(far)

    for h in range(heads):
        qf = feat(q_v[:, cols(h)].astype(F32))
        g_m = gate_of(h) * gm[:, cols(h)].astype(F32)
        rd = rdenom[h]
        g_n = (g_m * rd).astype(BF16)
        g_d = -jnp.sum(g_m * mem_out[:, cols(h)], -1, keepdims=True) * rd
        scan_put(1, h, dot_tn(qf.astype(BF16), g_n), jnp.sum(g_d * qf, 0, keepdims=True))
    scan_start(1)
    project(right, 1)
    rs_start(2, pf[1, half:rows, :])
    project(left, 2)
    rs_start(3, pf[2, 0:half, :])
    attention_back(0)
    attention_back(1)
    scan_middle(1)
    project(y, 3)
    attention_back(2)
    attention_back(3)
    rs[0].wait_recv()
    rs_start(4, pf[1, 0:half, :] + rs_dst[0].astype(F32))
    rs[1].wait_recv()
    rs_start(5, pf[2, half:rows, :] + rs_dst[1].astype(F32))
    scan_back(1)

    scan_end(1)
    for h in range(heads):
        memory, sums = scan_get(1, h)
        k_f = k_v[:, cols(h)].astype(F32)
        g_k = dot_nt(v_v[:, cols(h)], memory) + sums
        gk_v[:, cols(h)] = (kl[:, cols(h)] + g_k * slope(k_f)).astype(BF16)
        gv_v[:, cols(h)] = (vl[:, cols(h)] + dot_nn(feat(k_f).astype(BF16), memory)).astype(BF16)

    for i in range(2, 6):
        rs[i].wait_recv()
    out_v[0:half, :] = (
        pf[3, 0:half, :] + rs_dst[4].astype(F32) + rs_dst[3].astype(F32)
    ).astype(BF16)
    out_v[half:rows, :] = (
        pf[3, half:rows, :] + rs_dst[2].astype(F32) + rs_dst[5].astype(F32)
    ).astype(BF16)

    for copy in cot_out:
        copy.wait_send()
    for copy in rs:
        copy.wait_send()
    scan_sent(0)
    scan_sent(1)


def store(*refs):
    sources, targets, sem = refs[:4], refs[4:8], refs[8]
    copies = [
        pltpu.make_async_copy(src, dst, sem.at[i])
        for i, (src, dst) in enumerate(zip(sources, targets))
    ]
    for copy in copies:
        copy.start()
    for copy in copies:
        copy.wait()


def solution(mesh):
    split = Mesh(mesh.devices.reshape(8, 4, 2, mesh.shape["tp"]), SEQ_TP)
    zs, xs, cs, ts = split.devices.shape
    group = xs * cs

    def local(query, keys, values, beta, out_weight, cotangent):
        length, width = query.shape
        heads = width // HD
        rows, deep = cotangent.shape
        prow = heads * HD // group
        slab = prow + PAD
        vm = pltpu.VMEM
        dma = pltpu.SemaphoreType.DMA
        any_ = pl.BlockSpec(memory_space=pl.ANY)
        scratch = [
            vm((length, width), BF16), vm((length, width), BF16), vm((length, width), BF16),
            vm((width, deep), BF16), vm((ts, rows, deep), BF16), dma((5,)),
            dma((6,)), dma((6,)),
            vm((2, group, slab, HD), BF16), vm((2, group, slab, HD), BF16),
            vm((group, slab, HD), F32), vm((2, slab, HD), BF16), vm((slab, HD), F32),
            vm((2, zs, slab, HD), BF16),
            vm((2, group, slab, HD), BF16), vm((2, group, slab, HD), BF16),
            dma((2, 3, 8)), dma((2, 3, 8)),
            vm((heads, length, length), F32), vm((length, width), F32), vm((length, width), F32),
            vm((heads, length, 1), F32), vm((length, width), BF16), vm((length, width), BF16),
            vm((length, width), F32), vm((length, width), F32),
            vm((ts, rows, deep), F32), vm((6, rows // 2, deep), BF16), vm((6, rows // 2, deep), BF16),
            dma((6,)), dma((6,)),
        ]
        results = ((rows, deep), (length, width), (length, width), (length, width))
        held = pl.pallas_call(
            functools.partial(kernel, zs, xs, cs, ts),
            out_shape=tuple(vm(dims, BF16) for dims in results),
            in_specs=[any_, any_, any_, pl.BlockSpec(memory_space=pltpu.SMEM), any_, any_],
            out_specs=(pl.BlockSpec(memory_space=pltpu.VMEM),) * 4,
            scratch_shapes=scratch,
            compiler_params=pltpu.CompilerParams(
                collective_id=0, has_side_effects=True, vmem_limit_bytes=58 * 1024 * 1024
            ),
            cost_estimate=pl.CostEstimate(
                flops=5_000_000_000, bytes_accessed=8_000_000, transcendentals=2_000_000
            ),
            name="layer",
        )(query, keys, values, beta, out_weight, cotangent)
        return pl.pallas_call(
            store,
            out_shape=tuple(jax.ShapeDtypeStruct(dims, BF16) for dims in results),
            in_specs=[any_] * 4,
            out_specs=(any_,) * 4,
            scratch_shapes=[dma((4,))],
            compiler_params=pltpu.CompilerParams(vmem_limit_bytes=4 * 1024 * 1024),
            cost_estimate=pl.CostEstimate(flops=0, bytes_accessed=4_000_000, transcendentals=0),
            name="store",
        )(*held)

    placed = (P(SEQ, "tp"), P(SEQ, "tp"), P(SEQ, "tp"), P("tp"), P("tp", None), P(SEQ_TP, None))
    return jax.shard_map(
        local,
        mesh=split,
        in_specs=placed,
        out_specs=(P(SEQ_TP, None), P(SEQ, "tp"), P(SEQ, "tp"), P(SEQ, "tp")),
        check_vma=False,
    )
```

```python
import functools

import jax
import jax.numpy as jnp
from jax import lax
from jax.experimental import pallas as pl
from jax.experimental.pallas import tpu as pltpu
from jax.sharding import Mesh
from jax.sharding import PartitionSpec as P

HD = 128
SEQ = ("seq_0", "seq_1", "seq_2")
SEQ_TP = ("seq_0", "seq_1", "seq_2", "tp")
MESH = pl.DeviceIdType.MESH
F32 = jnp.float32
BF16 = jnp.bfloat16
BLOCK = 256
PAD = 16


def feat_slope(x):
    e = jnp.exp(jnp.minimum(x, 0.0))
    return jnp.where(x > 0, x + 1.0, e), jnp.where(x > 0, jnp.ones_like(x), e)


def by_distance(count, step):
    hops = {d: min(d // step, count // step - d // step) for d in range(1, count)}
    return sorted(hops, key=lambda d: -hops[d])


def dot_nn(a, b):
    return jnp.dot(a, b, preferred_element_type=F32)


def dot_nt(a, b):
    return lax.dot_general(a, b, (((1,), (1,)), ((), ())), preferred_element_type=F32)


def dot_tn(a, b):
    return lax.dot_general(a, b, (((0,), (0,)), ((), ())), preferred_element_type=F32)


def kernel(
    zs, xs, cs, ts,
    q_in, k_in, v_in, beta, w_in, cot_in,
    out_v, gq_v, gk_v, gv_v,
    q_v, k_v, v_v, w_v, cot_v, load_sem,
    cot_send, cot_recv,
    parcel, got1, part, total, base, got2, back, got3, all_sums,
    scan_send, scan_recv,
    probs, local_out, mem_out, rdenom, mixed, gm, kl, vl,
    kf_b, k_slope, q_feat, q_slope, grad_n, grad_d, grad_mem, grad_sum,
    pf, rs_src, rs_dst, rs_send, rs_recv,
):
    length, width = q_v.shape
    heads = width // HD
    rows = cot_in.shape[0]
    half = rows // 2
    group = xs * cs
    prow = parcel.shape[2] - PAD
    scale = HD ** (-0.5)

    z = lax.axis_index("seq_0")
    x = lax.axis_index("seq_1")
    c = lax.axis_index("seq_2")
    y = lax.axis_index("tp")
    g = x * cs + c
    right = lax.rem(y + 1, ts)
    left = lax.rem(y + ts - 1, ts)
    far = lax.rem(y + 2, ts)

    def at(x_=None, c_=None, z_=None, y_=None):
        return (
            z if z_ is None else z_,
            x if x_ is None else x_,
            c if c_ is None else c_,
            y if y_ is None else y_,
        )

    def member(p):
        return at(x_=p // cs, c_=lax.rem(p, cs))

    loads = []
    for i, (src, dst) in enumerate(
        ((k_in, k_v), (v_in, v_v), (q_in, q_v), (w_in, w_v), (cot_in, cot_v.at[y]))
    ):
        copy = pltpu.make_async_copy(src, dst, load_sem.at[i])
        copy.start()
        loads.append(copy)

    barrier = pltpu.get_barrier_semaphore()
    peers = [at(y_=left), at(y_=right)]
    peers += [member(lax.rem(g + d, group)) for d in range(1, group)]
    peers += [at(z_=lax.rem(z + d, zs)) for d in range(1, zs)]
    for peer in peers:
        pl.semaphore_signal(barrier, inc=1, device_id=peer, device_id_type=MESH)

    def remote(src, dst, send, recv, device):
        return pltpu.make_async_remote_copy(
            src_ref=src, dst_ref=dst, send_sem=send, recv_sem=recv,
            device_id=device, device_id_type=MESH,
        )

    first, second = pl.ds(0, half), pl.ds(half, half)

    def cot_copy(i, owner, part_, to, from_input):
        src = cot_in.at[part_] if from_input else cot_v.at[owner, part_]
        return remote(src, cot_v.at[owner, part_], cot_send.at[i], cot_recv.at[i], to)

    to_right, to_left = at(y_=right), at(y_=left)
    cot_out = [
        cot_copy(0, y, first, to_right, True),
        cot_copy(1, y, second, to_left, True),
        cot_copy(2, y, second, to_right, True),
        cot_copy(3, y, first, to_left, True),
        cot_copy(4, left, first, to_right, False),
        cot_copy(5, right, second, to_left, False),
    ]
    cot_arrive = [
        cot_copy(0, left, first, to_right, False),
        cot_copy(1, right, second, to_left, False),
        cot_copy(2, left, second, to_right, False),
        cot_copy(3, right, first, to_left, False),
        cot_copy(4, far, first, to_right, False),
        cot_copy(5, far, second, to_left, False),
    ]

    def cot_relay():
        for i in range(2):
            cot_arrive[i].wait_recv()
            cot_out[4 + i].start()

    def slices_out(s):
        return [
            remote(
                parcel.at[s, lax.rem(g + d, group)], got1.at[s, g],
                scan_send.at[s, 0, d], scan_recv.at[s, 0, d],
                member(lax.rem(g + d, group)),
            )
            for d in by_distance(group, cs)
        ]

    def slices_in(s):
        return [
            remote(
                parcel.at[s, g], got1.at[s, lax.rem(g + group - d, group)],
                scan_send.at[s, 0, d], scan_recv.at[s, 0, d],
                member(lax.rem(g + d, group)),
            )
            for d in by_distance(group, cs)
        ]

    def ahead(s, d):
        return z + d if s == 0 else z - d

    def behind(s, d):
        return z - d if s == 0 else z + d

    def inside(k):
        return jnp.logical_and(k >= 0, k < zs)

    def wrapped(k):
        return lax.rem(k + zs, zs)

    def total_out(s, d):
        return remote(
            total.at[s], got2.at[s, z], scan_send.at[s, 1, d], scan_recv.at[s, 1, d],
            at(z_=wrapped(ahead(s, d))),
        )

    def total_in(s, d):
        return remote(
            total.at[s], got2.at[s, wrapped(behind(s, d))],
            scan_send.at[s, 1, d], scan_recv.at[s, 1, d],
            at(z_=wrapped(ahead(s, d))),
        )

    def back_out(s):
        return [
            remote(
                back.at[s, lax.rem(g + d, group)], got3.at[s, g],
                scan_send.at[s, 2, d], scan_recv.at[s, 2, d],
                member(lax.rem(g + d, group)),
            )
            for d in by_distance(group, cs)
        ]

    def back_in(s):
        return [
            remote(
                back.at[s, g], got3.at[s, lax.rem(g + group - d, group)],
                scan_send.at[s, 2, d], scan_recv.at[s, 2, d],
                member(lax.rem(g + d, group)),
            )
            for d in by_distance(group, cs)
        ]

    def scan_put(s, memories, sums):
        rest = jnp.zeros((PAD - heads, HD), F32)
        wide = jnp.concatenate(sums + [rest], 0).astype(BF16)
        per = group // heads
        for h in range(heads):
            for j in range(per):
                piece = memories[h][j * prow : (j + 1) * prow]
                parcel[s, h * per + j, 0:prow, :] = piece.astype(BF16)
                parcel[s, h * per + j, prow : prow + PAD, :] = wide

    def scan_start(s):
        for copy in slices_out(s):
            copy.start()

    def scan_middle(s):
        got1[s, g] = parcel[s, g]
        for copy in slices_in(s):
            copy.wait_recv()
        run = jnp.zeros((prow + PAD, HD), F32)
        for p in range(group) if s == 0 else reversed(range(group)):
            part[p] = run
            run = run + got1[s, p].astype(F32)
        total[s] = run.astype(BF16)
        for d in by_distance(zs, 1):

            @pl.when(inside(ahead(s, d)))
            def _(d=d):
                total_out(s, d).start()

    def scan_back(s):
        base[...] = jnp.zeros_like(base)
        for d in by_distance(zs, 1):

            @pl.when(inside(behind(s, d)))
            def _(d=d):
                total_in(s, d).wait_recv()
                base[...] += got2[s, wrapped(behind(s, d))].astype(F32)

        for p in range(group):
            back[s, p] = (base[0:prow, :] + part[p, 0:prow, :]).astype(BF16)
        for copy in back_out(s):
            copy.start()
        got3[s, g] = back[s, g]
        all_sums[s] = base[prow : prow + PAD, :] + part[g, prow : prow + PAD, :]

    def scan_end(s):
        for copy in back_in(s):
            copy.wait_recv()

    def scan_memory(s, h):
        per = group // heads
        return jnp.concatenate([got3[s, h * per + j] for j in range(per)], 0)

    def scan_sums(s, h):
        return all_sums[s, h : h + 1, :]

    def scan_sent(s):
        for copy in slices_out(s):
            copy.wait_send()
        for d in by_distance(zs, 1):

            @pl.when(inside(ahead(s, d)))
            def _(d=d):
                total_out(s, d).wait_send()

        for copy in back_out(s):
            copy.wait_send()

    def cols(h):
        return pl.ds(h * HD, HD)

    def gate_of(h):
        return jax.nn.sigmoid(jnp.full((1, HD), beta[h], F32))

    blocks = length // BLOCK

    def attention(h):
        for i in range(blocks):
            q_rows, seen = pl.ds(i * BLOCK, BLOCK), pl.ds(0, (i + 1) * BLOCK)
            s_t = dot_nt(k_v[seen, cols(h)], q_v[q_rows, cols(h)]) * scale
            key_at = lax.broadcasted_iota(jnp.int32, s_t.shape, 0)
            query_at = lax.broadcasted_iota(jnp.int32, s_t.shape, 1) + i * BLOCK
            s_t = jnp.where(key_at <= query_at, s_t, -jnp.inf)
            e = jnp.exp(s_t - jnp.max(s_t, 0, keepdims=True))
            p = e * (1.0 / jnp.sum(e, 0, keepdims=True))
            probs[h, seen, q_rows] = p
            local_out[q_rows, cols(h)] = dot_tn(p.astype(BF16), v_v[seen, cols(h)])

    def attention_back(h):
        gate = gate_of(h)
        memory, sums = scan_memory(0, h), scan_sums(0, h)
        for i in reversed(range(blocks)):
            q_rows, seen = pl.ds(i * BLOCK, BLOCK), pl.ds(0, (i + 1) * BLOCK)
            g_f = gm[q_rows, cols(h)].astype(F32)
            g_l = ((1.0 - gate) * g_f).astype(BF16)
            q_b = q_v[q_rows, cols(h)]
            p = probs[h, seen, q_rows]
            gp = dot_nt(v_v[seen, cols(h)], g_l)
            delta = jnp.sum(p * gp, 0, keepdims=True)
            gs = (p * (gp - delta) * scale).astype(BF16)
            k_add, v_add = dot_nn(gs, q_b), dot_nn(p.astype(BF16), g_l)
            if i == blocks - 1:
                kl[seen, cols(h)] = k_add
                vl[seen, cols(h)] = v_add
            else:
                kl[seen, cols(h)] += k_add
                vl[seen, cols(h)] += v_add
            g_q = dot_nt(grad_n[q_rows, cols(h)], memory) + grad_d[h, q_rows, :] * sums
            own = dot_tn(gs, k_v[seen, cols(h)])
            gq_v[q_rows, cols(h)] = (own + g_q * q_slope[q_rows, cols(h)]).astype(BF16)

    loads[0].wait()
    loads[1].wait()
    memories, sums = [], []
    for h in range(heads):
        kf, k_slope[:, cols(h)] = feat_slope(k_v[:, cols(h)].astype(F32))
        kf_h = kf.astype(BF16)
        kf_b[:, cols(h)] = kf_h
        memories.append(dot_tn(kf_h, v_v[:, cols(h)]))
        sums.append(jnp.sum(kf, 0, keepdims=True))
    scan_put(0, memories, sums)
    pl.semaphore_wait(barrier, len(peers))
    for i in range(4):
        cot_out[i].start()
    scan_start(0)
    loads[2].wait()
    for h in range(heads):
        attention(h)
    scan_middle(0)
    cot_relay()

    def block_rows(b):
        return pl.ds(pl.multiple_of(b * rows, rows), rows)

    def grad_in(b):
        gm[block_rows(b), :] = dot_nt(cot_v[b], w_v[...]).astype(BF16)

    def project(b, slot):
        pf[slot] = dot_nn(mixed[block_rows(b), :], w_v[...])

    def rs_copy(i, to):
        return remote(rs_src.at[i], rs_dst.at[i], rs_send.at[i], rs_recv.at[i], to)

    rs = [rs_copy(i, to_right if i % 2 == 0 else to_left) for i in range(6)]

    def rs_start(i, piece):
        rs_src[i] = piece.astype(BF16)
        rs[i].start()

    loads[3].wait()
    loads[4].wait()
    grad_in(y)
    for h in range(heads):
        q_feat[:, cols(h)], q_slope[:, cols(h)] = feat_slope(q_v[:, cols(h)].astype(F32))
    scan_back(0)

    for h in range(heads):
        near = jnp.sum(q_feat[:, cols(h)] * scan_sums(0, h), -1, keepdims=True)
        rdenom[h] = 1.0 / (near + 1.0)

    def grad_block(b, start):
        part_rows = block_rows(b)
        for h in range(heads):
            g_m = gate_of(h) * gm[part_rows, cols(h)].astype(F32)
            g_n = (g_m * rdenom[h, part_rows, :]).astype(BF16)
            grad_n[part_rows, cols(h)] = g_n
            memory = dot_tn(q_feat[part_rows, cols(h)].astype(BF16), g_n)
            grad_mem[h] = memory if start else grad_mem[h] + memory

    def grad_row(b, start):
        part_rows = block_rows(b)
        for h in range(heads):
            g_m = gate_of(h) * gm[part_rows, cols(h)].astype(F32)
            over = jnp.sum(g_m * mem_out[part_rows, cols(h)], -1, keepdims=True)
            g_d = -over * rdenom[h, part_rows, :]
            grad_d[h, part_rows, :] = g_d
            total_d = jnp.sum(g_d * q_feat[part_rows, cols(h)], 0, keepdims=True)
            grad_sum[h] = total_d if start else grad_sum[h] + total_d

    grad_block(y, True)
    cot_arrive[2].wait_recv()
    grad_in(left)
    grad_block(left, False)
    cot_arrive[3].wait_recv()
    grad_in(right)
    grad_block(right, False)
    scan_end(0)

    def read_block(b):
        part_rows = block_rows(b)
        for h in range(heads):
            gate = gate_of(h)
            q_b = q_feat[part_rows, cols(h)].astype(BF16)
            m_o = dot_nn(q_b, scan_memory(0, h)) * rdenom[h, part_rows, :]
            mem_out[part_rows, cols(h)] = m_o
            mix = gate * m_o + (1.0 - gate) * local_out[part_rows, cols(h)]
            mixed[part_rows, cols(h)] = mix.astype(BF16)

    read_block(far)
    project(far, 0)
    rs_start(0, pf[0, 0:half, :])
    rs_start(1, pf[0, half:rows, :])
    read_block(right)
    project(right, 1)
    rs_start(2, pf[1, half:rows, :])
    read_block(left)
    project(left, 2)
    rs_start(3, pf[2, 0:half, :])
    read_block(y)
    grad_row(y, True)
    grad_row(left, False)
    grad_row(right, False)
    cot_arrive[4].wait_recv()
    cot_arrive[5].wait_recv()
    grad_in(far)
    grad_block(far, False)
    grad_row(far, False)
    scan_put(1, [grad_mem[h] for h in range(heads)], [grad_sum[h] for h in range(heads)])
    scan_start(1)
    attention_back(0)
    attention_back(1)
    scan_middle(1)
    rs[0].wait_recv()
    rs_start(4, pf[1, 0:half, :] + rs_dst[0].astype(F32))
    rs[1].wait_recv()
    rs_start(5, pf[2, half:rows, :] + rs_dst[1].astype(F32))
    project(y, 3)
    attention_back(2)
    attention_back(3)
    scan_back(1)

    scan_end(1)
    for h in range(heads):
        memory, sums = scan_memory(1, h), scan_sums(1, h)
        g_k = dot_nt(v_v[:, cols(h)], memory) + sums
        gk_v[:, cols(h)] = (kl[:, cols(h)] + g_k * k_slope[:, cols(h)]).astype(BF16)
        gv_v[:, cols(h)] = (vl[:, cols(h)] + dot_nn(kf_b[:, cols(h)], memory)).astype(BF16)

    for i in range(2, 6):
        rs[i].wait_recv()
    out_v[0:half, :] = (
        pf[3, 0:half, :] + rs_dst[4].astype(F32) + rs_dst[3].astype(F32)
    ).astype(BF16)
    out_v[half:rows, :] = (
        pf[3, half:rows, :] + rs_dst[2].astype(F32) + rs_dst[5].astype(F32)
    ).astype(BF16)

    for copy in cot_out:
        copy.wait_send()
    for copy in rs:
        copy.wait_send()
    scan_sent(0)
    scan_sent(1)


def store(*refs):
    sources, targets, sem = refs[:4], refs[4:8], refs[8]
    copies = [
        pltpu.make_async_copy(src, dst, sem.at[i])
        for i, (src, dst) in enumerate(zip(sources, targets))
    ]
    for copy in copies:
        copy.start()
    for copy in copies:
        copy.wait()


def solution(mesh):
    split = Mesh(mesh.devices.reshape(8, 4, 2, mesh.shape["tp"]), SEQ_TP)
    zs, xs, cs, ts = split.devices.shape
    group = xs * cs

    def local(query, keys, values, beta, out_weight, cotangent):
        length, width = query.shape
        heads = width // HD
        rows, deep = cotangent.shape
        prow = heads * HD // group
        slab = prow + PAD
        vm = pltpu.VMEM
        dma = pltpu.SemaphoreType.DMA
        any_ = pl.BlockSpec(memory_space=pl.ANY)
        scratch = [
            vm((length, width), BF16), vm((length, width), BF16), vm((length, width), BF16),
            vm((width, deep), BF16), vm((ts, rows, deep), BF16), dma((5,)),
            dma((6,)), dma((6,)),
            vm((2, group, slab, HD), BF16), vm((2, group, slab, HD), BF16),
            vm((group, slab, HD), F32), vm((2, slab, HD), BF16), vm((slab, HD), F32),
            vm((2, zs, slab, HD), BF16),
            vm((2, group, prow, HD), BF16), vm((2, group, prow, HD), BF16), vm((2, PAD, HD), F32),
            dma((2, 3, 8)), dma((2, 3, 8)),
            vm((heads, length, length), F32), vm((length, width), F32), vm((length, width), F32),
            vm((heads, length, 1), F32), vm((length, width), BF16), vm((length, width), BF16),
            vm((length, width), F32), vm((length, width), F32),
            vm((length, width), BF16), vm((length, width), F32), vm((length, width), F32),
            vm((length, width), F32), vm((length, width), BF16), vm((heads, length, 1), F32),
            vm((heads, HD, HD), F32), vm((heads, 1, HD), F32),
            vm((ts, rows, deep), F32), vm((6, rows // 2, deep), BF16), vm((6, rows // 2, deep), BF16),
            dma((6,)), dma((6,)),
        ]
        results = ((rows, deep), (length, width), (length, width), (length, width))
        held = pl.pallas_call(
            functools.partial(kernel, zs, xs, cs, ts),
            out_shape=tuple(vm(dims, BF16) for dims in results),
            in_specs=[any_, any_, any_, pl.BlockSpec(memory_space=pltpu.SMEM), any_, any_],
            out_specs=(pl.BlockSpec(memory_space=pltpu.VMEM),) * 4,
            scratch_shapes=scratch,
            compiler_params=pltpu.CompilerParams(
                collective_id=0, has_side_effects=True, vmem_limit_bytes=58 * 1024 * 1024
            ),
            cost_estimate=pl.CostEstimate(
                flops=5_000_000_000, bytes_accessed=8_000_000, transcendentals=2_000_000
            ),
            name="layer",
        )(query, keys, values, beta, out_weight, cotangent)
        return pl.pallas_call(
            store,
            out_shape=tuple(jax.ShapeDtypeStruct(dims, BF16) for dims in results),
            in_specs=[any_] * 4,
            out_specs=(any_,) * 4,
            scratch_shapes=[dma((4,))],
            compiler_params=pltpu.CompilerParams(vmem_limit_bytes=4 * 1024 * 1024),
            cost_estimate=pl.CostEstimate(flops=0, bytes_accessed=4_000_000, transcendentals=0),
            name="store",
        )(*held)

    placed = (P(SEQ, "tp"), P(SEQ, "tp"), P(SEQ, "tp"), P("tp"), P("tp", None), P(SEQ_TP, None))
    return jax.shard_map(
        local,
        mesh=split,
        in_specs=placed,
        out_specs=(P(SEQ_TP, None), P(SEQ, "tp"), P(SEQ, "tp"), P(SEQ, "tp")),
        check_vma=False,
    )
```

```python
import functools

import jax
import jax.numpy as jnp
from jax import lax
from jax.experimental import pallas as pl
from jax.experimental.pallas import tpu as pltpu
from jax.sharding import Mesh
from jax.sharding import PartitionSpec as P

HD = 128
SEQ = ("seq_0", "seq_1", "seq_2")
SEQ_TP = ("seq_0", "seq_1", "seq_2", "tp")
MESH = pl.DeviceIdType.MESH
F32 = jnp.float32
BF16 = jnp.bfloat16
BLOCK = 256
PAD = 16


def feat_slope(x):
    e = jnp.exp(jnp.minimum(x, 0.0))
    return jnp.where(x > 0, x + 1.0, e), jnp.where(x > 0, jnp.ones_like(x), e)


def by_distance(count, step):
    hops = {d: min(d // step, count // step - d // step) for d in range(1, count)}
    return sorted(hops, key=lambda d: -hops[d])


def dot_nn(a, b):
    return jnp.dot(a, b, preferred_element_type=F32)


def dot_nt(a, b):
    return lax.dot_general(a, b, (((1,), (1,)), ((), ())), preferred_element_type=F32)


def dot_tn(a, b):
    return lax.dot_general(a, b, (((0,), (0,)), ((), ())), preferred_element_type=F32)


def kernel(
    zs, xs, cs, ts,
    q_in, k_in, v_in, beta, w_in, cot_in,
    out_v, gq_v, gk_v, gv_v,
    q_v, k_v, v_v, w_v, cot_v, load_sem,
    cot_send, cot_recv,
    parcel, got1, part, total, base, got2, back, got3, all_sums,
    scan_send, scan_recv,
    probs, local_out, mem_out, rdenom, mixed, gm, kl, vl,
    kf_b, k_slope, q_feat, q_slope, grad_n, grad_d, grad_mem, grad_sum,
    pf, rs_src, rs_dst, rs_send, rs_recv,
):
    length, width = q_v.shape
    heads = width // HD
    rows = cot_in.shape[0]
    half = rows // 2
    group = xs * cs
    prow = parcel.shape[2] - PAD
    scale = HD ** (-0.5)

    z = lax.axis_index("seq_0")
    x = lax.axis_index("seq_1")
    c = lax.axis_index("seq_2")
    y = lax.axis_index("tp")
    g = x * cs + c
    right = lax.rem(y + 1, ts)
    left = lax.rem(y + ts - 1, ts)
    far = lax.rem(y + 2, ts)

    def at(x_=None, c_=None, z_=None, y_=None):
        return (
            z if z_ is None else z_,
            x if x_ is None else x_,
            c if c_ is None else c_,
            y if y_ is None else y_,
        )

    def member(p):
        return at(x_=p // cs, c_=lax.rem(p, cs))

    barrier = pltpu.get_barrier_semaphore()
    peers = [at(z_=lax.rem(z + d, zs)) for d in by_distance(zs, 1)]
    peers += [member(lax.rem(g + d, group)) for d in by_distance(group, cs)]
    peers += [at(y_=left), at(y_=right)]
    for peer in peers:
        pl.semaphore_signal(barrier, inc=1, device_id=peer, device_id_type=MESH)

    loads = []
    for i, (src, dst) in enumerate(
        ((k_in, k_v), (v_in, v_v), (q_in, q_v), (w_in, w_v), (cot_in, cot_v.at[y]))
    ):
        copy = pltpu.make_async_copy(src, dst, load_sem.at[i])
        copy.start()
        loads.append(copy)

    def remote(src, dst, send, recv, device):
        return pltpu.make_async_remote_copy(
            src_ref=src, dst_ref=dst, send_sem=send, recv_sem=recv,
            device_id=device, device_id_type=MESH,
        )

    first, second = pl.ds(0, half), pl.ds(half, half)

    def cot_copy(i, owner, part_, to, from_input):
        src = cot_in.at[part_] if from_input else cot_v.at[owner, part_]
        return remote(src, cot_v.at[owner, part_], cot_send.at[i], cot_recv.at[i], to)

    to_right, to_left = at(y_=right), at(y_=left)
    cot_out = [
        cot_copy(0, y, first, to_right, True),
        cot_copy(1, y, second, to_left, True),
        cot_copy(2, y, second, to_right, True),
        cot_copy(3, y, first, to_left, True),
        cot_copy(4, left, first, to_right, False),
        cot_copy(5, right, second, to_left, False),
    ]
    cot_arrive = [
        cot_copy(0, left, first, to_right, False),
        cot_copy(1, right, second, to_left, False),
        cot_copy(2, left, second, to_right, False),
        cot_copy(3, right, first, to_left, False),
        cot_copy(4, far, first, to_right, False),
        cot_copy(5, far, second, to_left, False),
    ]

    def cot_relay():
        for i in range(2):
            cot_arrive[i].wait_recv()
            cot_out[4 + i].start()

    def slices_out(s):
        return [
            remote(
                parcel.at[s, lax.rem(g + d, group)], got1.at[s, g],
                scan_send.at[s, 0, d], scan_recv.at[s, 0, d],
                member(lax.rem(g + d, group)),
            )
            for d in by_distance(group, cs)
        ]

    def slices_in(s):
        return [
            remote(
                parcel.at[s, g], got1.at[s, lax.rem(g + group - d, group)],
                scan_send.at[s, 0, d], scan_recv.at[s, 0, d],
                member(lax.rem(g + d, group)),
            )
            for d in by_distance(group, cs)
        ]

    def ahead(s, d):
        return z + d if s == 0 else z - d

    def behind(s, d):
        return z - d if s == 0 else z + d

    def inside(k):
        return jnp.logical_and(k >= 0, k < zs)

    def wrapped(k):
        return lax.rem(k + zs, zs)

    def total_out(s, d):
        return remote(
            total.at[s], got2.at[s, z], scan_send.at[s, 1, d], scan_recv.at[s, 1, d],
            at(z_=wrapped(ahead(s, d))),
        )

    def total_in(s, d):
        return remote(
            total.at[s], got2.at[s, wrapped(behind(s, d))],
            scan_send.at[s, 1, d], scan_recv.at[s, 1, d],
            at(z_=wrapped(ahead(s, d))),
        )

    def back_out(s):
        return [
            remote(
                back.at[s, lax.rem(g + d, group)], got3.at[s, g],
                scan_send.at[s, 2, d], scan_recv.at[s, 2, d],
                member(lax.rem(g + d, group)),
            )
            for d in by_distance(group, cs)
        ]

    def back_in(s):
        return [
            remote(
                back.at[s, g], got3.at[s, lax.rem(g + group - d, group)],
                scan_send.at[s, 2, d], scan_recv.at[s, 2, d],
                member(lax.rem(g + d, group)),
            )
            for d in by_distance(group, cs)
        ]

    def scan_put(s, memories, sums):
        rest = jnp.zeros((PAD - heads, HD), F32)
        wide = jnp.concatenate(sums + [rest], 0).astype(BF16)
        per = group // heads
        for h in range(heads):
            for j in range(per):
                piece = memories[h][j * prow : (j + 1) * prow]
                parcel[s, h * per + j, 0:prow, :] = piece.astype(BF16)
                parcel[s, h * per + j, prow : prow + PAD, :] = wide

    def scan_start(s):
        for copy in slices_out(s):
            copy.start()

    def scan_middle(s):
        got1[s, g] = parcel[s, g]
        for copy in slices_in(s):
            copy.wait_recv()
        run = jnp.zeros((prow + PAD, HD), F32)
        for p in range(group) if s == 0 else reversed(range(group)):
            part[p] = run
            run = run + got1[s, p].astype(F32)
        total[s] = run.astype(BF16)
        for d in by_distance(zs, 1):

            @pl.when(inside(ahead(s, d)))
            def _(d=d):
                total_out(s, d).start()

    def scan_back(s):
        base[...] = jnp.zeros_like(base)
        for d in by_distance(zs, 1):

            @pl.when(inside(behind(s, d)))
            def _(d=d):
                total_in(s, d).wait_recv()
                base[...] += got2[s, wrapped(behind(s, d))].astype(F32)

        for p in range(group):
            back[s, p] = (base[0:prow, :] + part[p, 0:prow, :]).astype(BF16)
        for copy in back_out(s):
            copy.start()
        got3[s, g] = back[s, g]
        all_sums[s] = base[prow : prow + PAD, :] + part[g, prow : prow + PAD, :]

    def scan_end(s):
        for copy in back_in(s):
            copy.wait_recv()

    def scan_memory(s, h):
        per = group // heads
        return jnp.concatenate([got3[s, h * per + j] for j in range(per)], 0)

    def scan_sums(s, h):
        return all_sums[s, h : h + 1, :]

    def scan_sent(s):
        for copy in slices_out(s):
            copy.wait_send()
        for d in by_distance(zs, 1):

            @pl.when(inside(ahead(s, d)))
            def _(d=d):
                total_out(s, d).wait_send()

        for copy in back_out(s):
            copy.wait_send()

    def cols(h):
        return pl.ds(h * HD, HD)

    def gate_of(h):
        return jax.nn.sigmoid(jnp.full((1, HD), beta[h], F32))

    blocks = length // BLOCK

    def attention(h):
        for i in range(blocks):
            q_rows, seen = pl.ds(i * BLOCK, BLOCK), pl.ds(0, (i + 1) * BLOCK)
            s_t = dot_nt(k_v[seen, cols(h)], q_v[q_rows, cols(h)]) * scale
            key_at = lax.broadcasted_iota(jnp.int32, s_t.shape, 0)
            query_at = lax.broadcasted_iota(jnp.int32, s_t.shape, 1) + i * BLOCK
            s_t = jnp.where(key_at <= query_at, s_t, -jnp.inf)
            e = jnp.exp(s_t - jnp.max(s_t, 0, keepdims=True))
            p = e * (1.0 / jnp.sum(e, 0, keepdims=True))
            probs[h, seen, q_rows] = p
            local_out[q_rows, cols(h)] = dot_tn(p.astype(BF16), v_v[seen, cols(h)])

    def attention_back(h):
        gate = gate_of(h)
        memory, sums = scan_memory(0, h), scan_sums(0, h)
        for i in reversed(range(blocks)):
            q_rows, seen = pl.ds(i * BLOCK, BLOCK), pl.ds(0, (i + 1) * BLOCK)
            g_f = gm[q_rows, cols(h)].astype(F32)
            g_l = ((1.0 - gate) * g_f).astype(BF16)
            q_b = q_v[q_rows, cols(h)]
            p = probs[h, seen, q_rows]
            gp = dot_nt(v_v[seen, cols(h)], g_l)
            delta = jnp.sum(p * gp, 0, keepdims=True)
            gs = (p * (gp - delta) * scale).astype(BF16)
            k_add, v_add = dot_nn(gs, q_b), dot_nn(p.astype(BF16), g_l)
            if i == blocks - 1:
                kl[seen, cols(h)] = k_add
                vl[seen, cols(h)] = v_add
            else:
                kl[seen, cols(h)] += k_add
                vl[seen, cols(h)] += v_add
            g_q = dot_nt(grad_n[q_rows, cols(h)], memory) + grad_d[h, q_rows, :] * sums
            own = dot_tn(gs, k_v[seen, cols(h)])
            gq_v[q_rows, cols(h)] = (own + g_q * q_slope[q_rows, cols(h)]).astype(BF16)

    loads[0].wait()
    loads[1].wait()
    memories, sums = [], []
    for h in range(heads):
        if h == 2:
            pl.semaphore_wait(barrier, len(peers))
            for i in range(4):
                cot_out[i].start()
        kf, k_slope[:, cols(h)] = feat_slope(k_v[:, cols(h)].astype(F32))
        kf_h = kf.astype(BF16)
        kf_b[:, cols(h)] = kf_h
        memories.append(dot_tn(kf_h, v_v[:, cols(h)]))
        sums.append(jnp.sum(kf, 0, keepdims=True))
    scan_put(0, memories, sums)
    scan_start(0)
    loads[2].wait()
    for h in range(heads):
        attention(h)
    scan_middle(0)
    cot_relay()

    def block_rows(b):
        return pl.ds(pl.multiple_of(b * rows, rows), rows)

    def grad_in(b):
        gm[block_rows(b), :] = dot_nt(cot_v[b], w_v[...]).astype(BF16)

    def project(b, slot):
        pf[slot] = dot_nn(mixed[block_rows(b), :], w_v[...])

    def rs_copy(i, to):
        return remote(rs_src.at[i], rs_dst.at[i], rs_send.at[i], rs_recv.at[i], to)

    rs = [rs_copy(i, to_right if i % 2 == 0 else to_left) for i in range(6)]

    def rs_start(i, piece):
        rs_src[i] = piece.astype(BF16)
        rs[i].start()

    loads[3].wait()
    loads[4].wait()
    grad_in(y)
    for h in range(heads):
        q_feat[:, cols(h)], q_slope[:, cols(h)] = feat_slope(q_v[:, cols(h)].astype(F32))
    scan_back(0)

    for h in range(heads):
        near = jnp.sum(q_feat[:, cols(h)] * scan_sums(0, h), -1, keepdims=True)
        rdenom[h] = 1.0 / (near + 1.0)

    def grad_block(b, start):
        part_rows = block_rows(b)
        for h in range(heads):
            g_m = gate_of(h) * gm[part_rows, cols(h)].astype(F32)
            g_n = (g_m * rdenom[h, part_rows, :]).astype(BF16)
            grad_n[part_rows, cols(h)] = g_n
            memory = dot_tn(q_feat[part_rows, cols(h)].astype(BF16), g_n)
            grad_mem[h] = memory if start else grad_mem[h] + memory

    def grad_row(b, start):
        part_rows = block_rows(b)
        for h in range(heads):
            g_m = gate_of(h) * gm[part_rows, cols(h)].astype(F32)
            over = jnp.sum(g_m * mem_out[part_rows, cols(h)], -1, keepdims=True)
            g_d = -over * rdenom[h, part_rows, :]
            grad_d[h, part_rows, :] = g_d
            total_d = jnp.sum(g_d * q_feat[part_rows, cols(h)], 0, keepdims=True)
            grad_sum[h] = total_d if start else grad_sum[h] + total_d

    grad_block(y, True)
    cot_arrive[2].wait_recv()
    grad_in(left)
    grad_block(left, False)
    cot_arrive[3].wait_recv()
    grad_in(right)
    grad_block(right, False)
    scan_end(0)

    def read_block(b):
        part_rows = block_rows(b)
        for h in range(heads):
            gate = gate_of(h)
            q_b = q_feat[part_rows, cols(h)].astype(BF16)
            m_o = dot_nn(q_b, scan_memory(0, h)) * rdenom[h, part_rows, :]
            mem_out[part_rows, cols(h)] = m_o
            mix = gate * m_o + (1.0 - gate) * local_out[part_rows, cols(h)]
            mixed[part_rows, cols(h)] = mix.astype(BF16)

    read_block(far)
    project(far, 0)
    rs_start(0, pf[0, 0:half, :])
    rs_start(1, pf[0, half:rows, :])
    read_block(right)
    read_block(left)
    read_block(y)
    grad_row(y, True)
    grad_row(left, False)
    grad_row(right, False)
    cot_arrive[4].wait_recv()
    cot_arrive[5].wait_recv()
    grad_in(far)
    grad_block(far, False)
    grad_row(far, False)
    scan_put(1, [grad_mem[h] for h in range(heads)], [grad_sum[h] for h in range(heads)])
    scan_start(1)
    project(right, 1)
    rs_start(2, pf[1, half:rows, :])
    project(left, 2)
    rs_start(3, pf[2, 0:half, :])
    attention_back(0)
    scan_middle(1)
    attention_back(1)
    attention_back(2)
    rs[0].wait_recv()
    rs_start(4, pf[1, 0:half, :] + rs_dst[0].astype(F32))
    rs[1].wait_recv()
    rs_start(5, pf[2, half:rows, :] + rs_dst[1].astype(F32))
    scan_back(1)
    attention_back(3)
    project(y, 3)
    scan_end(1)
    for h in range(heads):
        memory, sums = scan_memory(1, h), scan_sums(1, h)
        g_k = dot_nt(v_v[:, cols(h)], memory) + sums
        gk_v[:, cols(h)] = (kl[:, cols(h)] + g_k * k_slope[:, cols(h)]).astype(BF16)
        gv_v[:, cols(h)] = (vl[:, cols(h)] + dot_nn(kf_b[:, cols(h)], memory)).astype(BF16)

    for i in range(2, 6):
        rs[i].wait_recv()
    out_v[0:half, :] = (
        pf[3, 0:half, :] + rs_dst[4].astype(F32) + rs_dst[3].astype(F32)
    ).astype(BF16)
    out_v[half:rows, :] = (
        pf[3, half:rows, :] + rs_dst[2].astype(F32) + rs_dst[5].astype(F32)
    ).astype(BF16)

    for copy in cot_out:
        copy.wait_send()
    for copy in rs:
        copy.wait_send()
    scan_sent(0)
    scan_sent(1)


def store(*refs):
    sources, targets, sem = refs[:4], refs[4:8], refs[8]
    copies = [
        pltpu.make_async_copy(src, dst, sem.at[i])
        for i, (src, dst) in enumerate(zip(sources, targets))
    ]
    for copy in copies:
        copy.start()
    for copy in copies:
        copy.wait()


def solution(mesh):
    split = Mesh(mesh.devices.reshape(8, 4, 2, mesh.shape["tp"]), SEQ_TP)
    zs, xs, cs, ts = split.devices.shape
    group = xs * cs

    def local(query, keys, values, beta, out_weight, cotangent):
        length, width = query.shape
        heads = width // HD
        rows, deep = cotangent.shape
        prow = heads * HD // group
        slab = prow + PAD
        vm = pltpu.VMEM
        dma = pltpu.SemaphoreType.DMA
        any_ = pl.BlockSpec(memory_space=pl.ANY)
        scratch = [
            vm((length, width), BF16), vm((length, width), BF16), vm((length, width), BF16),
            vm((width, deep), BF16), vm((ts, rows, deep), BF16), dma((5,)),
            dma((6,)), dma((6,)),
            vm((2, group, slab, HD), BF16), vm((2, group, slab, HD), BF16),
            vm((group, slab, HD), F32), vm((2, slab, HD), BF16), vm((slab, HD), F32),
            vm((2, zs, slab, HD), BF16),
            vm((2, group, prow, HD), BF16), vm((2, group, prow, HD), BF16), vm((2, PAD, HD), F32),
            dma((2, 3, 8)), dma((2, 3, 8)),
            vm((heads, length, length), F32), vm((length, width), F32), vm((length, width), F32),
            vm((heads, length, 1), F32), vm((length, width), BF16), vm((length, width), BF16),
            vm((length, width), F32), vm((length, width), F32),
            vm((length, width), BF16), vm((length, width), F32), vm((length, width), F32),
            vm((length, width), F32), vm((length, width), BF16), vm((heads, length, 1), F32),
            vm((heads, HD, HD), F32), vm((heads, 1, HD), F32),
            vm((ts, rows, deep), F32), vm((6, rows // 2, deep), BF16), vm((6, rows // 2, deep), BF16),
            dma((6,)), dma((6,)),
        ]
        results = ((rows, deep), (length, width), (length, width), (length, width))
        held = pl.pallas_call(
            functools.partial(kernel, zs, xs, cs, ts),
            out_shape=tuple(vm(dims, BF16) for dims in results),
            in_specs=[any_, any_, any_, pl.BlockSpec(memory_space=pltpu.SMEM), any_, any_],
            out_specs=(pl.BlockSpec(memory_space=pltpu.VMEM),) * 4,
            scratch_shapes=scratch,
            compiler_params=pltpu.CompilerParams(
                collective_id=0, has_side_effects=True, vmem_limit_bytes=58 * 1024 * 1024
            ),
            cost_estimate=pl.CostEstimate(
                flops=5_000_000_000, bytes_accessed=8_000_000, transcendentals=2_000_000
            ),
            name="layer",
        )(query, keys, values, beta, out_weight, cotangent)
        return pl.pallas_call(
            store,
            out_shape=tuple(jax.ShapeDtypeStruct(dims, BF16) for dims in results),
            in_specs=[any_] * 4,
            out_specs=(any_,) * 4,
            scratch_shapes=[dma((4,))],
            compiler_params=pltpu.CompilerParams(vmem_limit_bytes=4 * 1024 * 1024),
            cost_estimate=pl.CostEstimate(flops=0, bytes_accessed=4_000_000, transcendentals=0),
            name="store",
        )(*held)

    placed = (P(SEQ, "tp"), P(SEQ, "tp"), P(SEQ, "tp"), P("tp"), P("tp", None), P(SEQ_TP, None))
    return jax.shard_map(
        local,
        mesh=split,
        in_specs=placed,
        out_specs=(P(SEQ_TP, None), P(SEQ, "tp"), P(SEQ, "tp"), P(SEQ, "tp")),
        check_vma=False,
    )
```

```python
import functools

import jax
import jax.numpy as jnp
from jax import lax
from jax.experimental import pallas as pl
from jax.experimental.pallas import tpu as pltpu
from jax.sharding import Mesh
from jax.sharding import PartitionSpec as P

HD = 128
SEQ = ("seq_0", "seq_1", "seq_2")
SEQ_TP = ("seq_0", "seq_1", "seq_2", "tp")
MESH = pl.DeviceIdType.MESH
F32 = jnp.float32
BF16 = jnp.bfloat16
BLOCK = 256
PAD = 16


def feat_slope(x):
    e = jnp.exp(jnp.minimum(x, 0.0))
    return jnp.where(x > 0, x + 1.0, e), jnp.where(x > 0, jnp.ones_like(x), e)


def by_distance(count, step):
    hops = {d: min(d // step, count // step - d // step) for d in range(1, count)}
    return sorted(hops, key=lambda d: -hops[d])


def dot_nn(a, b):
    return jnp.dot(a, b, preferred_element_type=F32)


def dot_nt(a, b):
    return lax.dot_general(a, b, (((1,), (1,)), ((), ())), preferred_element_type=F32)


def dot_tn(a, b):
    return lax.dot_general(a, b, (((0,), (0,)), ((), ())), preferred_element_type=F32)


def kernel(
    zs, xs, cs, ts,
    q_in, k_in, v_in, beta, w_in, cot_in,
    out_v, gq_v, gk_v, gv_v,
    q_v, k_v, v_v, w_v, cot_v, load_sem,
    cot_send, cot_recv,
    parcel, got1, part, total, base, got2, back, got3, all_sums,
    scan_send, scan_recv,
    probs, local_out, mem_out, rdenom, mixed, gm, kl, vl,
    kf_b, k_slope, q_feat, q_slope, grad_n, grad_d, grad_mem, grad_sum,
    pf, rs_src, rs_dst, rs_send, rs_recv,
):
    length, width = q_v.shape
    heads = width // HD
    rows = cot_in.shape[0]
    half = rows // 2
    group = xs * cs
    prow = parcel.shape[2] - PAD
    scale = HD ** (-0.5)

    z = lax.axis_index("seq_0")
    x = lax.axis_index("seq_1")
    c = lax.axis_index("seq_2")
    y = lax.axis_index("tp")
    g = x * cs + c
    right = lax.rem(y + 1, ts)
    left = lax.rem(y + ts - 1, ts)
    far = lax.rem(y + 2, ts)

    def at(x_=None, c_=None, z_=None, y_=None):
        return (
            z if z_ is None else z_,
            x if x_ is None else x_,
            c if c_ is None else c_,
            y if y_ is None else y_,
        )

    def member(p):
        return at(x_=p // cs, c_=lax.rem(p, cs))

    barrier = pltpu.get_barrier_semaphore()
    peers = [at(z_=lax.rem(z + d, zs)) for d in by_distance(zs, 1)]
    peers += [member(lax.rem(g + d, group)) for d in by_distance(group, cs)]
    peers += [at(y_=left), at(y_=right)]
    for peer in peers:
        pl.semaphore_signal(barrier, inc=1, device_id=peer, device_id_type=MESH)

    loads = []
    for i, (src, dst) in enumerate(
        ((k_in, k_v), (v_in, v_v), (q_in, q_v), (w_in, w_v), (cot_in, cot_v.at[y]))
    ):
        copy = pltpu.make_async_copy(src, dst, load_sem.at[i])
        copy.start()
        loads.append(copy)

    def remote(src, dst, send, recv, device):
        return pltpu.make_async_remote_copy(
            src_ref=src, dst_ref=dst, send_sem=send, recv_sem=recv,
            device_id=device, device_id_type=MESH,
        )

    first, second = pl.ds(0, half), pl.ds(half, half)

    def cot_copy(i, owner, part_, to, from_input):
        src = cot_in.at[part_] if from_input else cot_v.at[owner, part_]
        return remote(src, cot_v.at[owner, part_], cot_send.at[i], cot_recv.at[i], to)

    to_right, to_left = at(y_=right), at(y_=left)
    cot_out = [
        cot_copy(0, y, first, to_right, True),
        cot_copy(1, y, second, to_left, True),
        cot_copy(2, y, second, to_right, True),
        cot_copy(3, y, first, to_left, True),
        cot_copy(4, left, first, to_right, False),
        cot_copy(5, right, second, to_left, False),
    ]
    cot_arrive = [
        cot_copy(0, left, first, to_right, False),
        cot_copy(1, right, second, to_left, False),
        cot_copy(2, left, second, to_right, False),
        cot_copy(3, right, first, to_left, False),
        cot_copy(4, far, first, to_right, False),
        cot_copy(5, far, second, to_left, False),
    ]

    def cot_relay():
        for i in range(2):
            cot_arrive[i].wait_recv()
            cot_out[4 + i].start()

    def slices_out(s):
        return [
            remote(
                parcel.at[s, lax.rem(g + d, group)], got1.at[s, g],
                scan_send.at[s, 0, d], scan_recv.at[s, 0, d],
                member(lax.rem(g + d, group)),
            )
            for d in by_distance(group, cs)
        ]

    def slices_in(s):
        return [
            remote(
                parcel.at[s, g], got1.at[s, lax.rem(g + group - d, group)],
                scan_send.at[s, 0, d], scan_recv.at[s, 0, d],
                member(lax.rem(g + d, group)),
            )
            for d in by_distance(group, cs)
        ]

    def ahead(s, d):
        return z + d if s == 0 else z - d

    def behind(s, d):
        return z - d if s == 0 else z + d

    def inside(k):
        return jnp.logical_and(k >= 0, k < zs)

    def wrapped(k):
        return lax.rem(k + zs, zs)

    def total_out(s, d):
        return remote(
            total.at[s], got2.at[s, z], scan_send.at[s, 1, d], scan_recv.at[s, 1, d],
            at(z_=wrapped(ahead(s, d))),
        )

    def total_in(s, d):
        return remote(
            total.at[s], got2.at[s, wrapped(behind(s, d))],
            scan_send.at[s, 1, d], scan_recv.at[s, 1, d],
            at(z_=wrapped(ahead(s, d))),
        )

    def back_out(s):
        return [
            remote(
                back.at[s, lax.rem(g + d, group)], got3.at[s, g],
                scan_send.at[s, 2, d], scan_recv.at[s, 2, d],
                member(lax.rem(g + d, group)),
            )
            for d in by_distance(group, cs)
        ]

    def back_in(s):
        return [
            remote(
                back.at[s, g], got3.at[s, lax.rem(g + group - d, group)],
                scan_send.at[s, 2, d], scan_recv.at[s, 2, d],
                member(lax.rem(g + d, group)),
            )
            for d in by_distance(group, cs)
        ]

    def scan_put(s, memories, sums):
        rest = jnp.zeros((PAD - heads, HD), F32)
        wide = jnp.concatenate(sums + [rest], 0).astype(BF16)
        per = group // heads
        for h in range(heads):
            for j in range(per):
                piece = memories[h][j * prow : (j + 1) * prow]
                parcel[s, h * per + j, 0:prow, :] = piece.astype(BF16)
                parcel[s, h * per + j, prow : prow + PAD, :] = wide

    def scan_start(s):
        for copy in slices_out(s):
            copy.start()

    def scan_middle(s):
        got1[s, g] = parcel[s, g]
        for copy in slices_in(s):
            copy.wait_recv()
        run = jnp.zeros((prow + PAD, HD), F32)
        for p in range(group) if s == 0 else reversed(range(group)):
            part[p] = run
            run = run + got1[s, p].astype(F32)
        total[s] = run.astype(BF16)
        for d in by_distance(zs, 1):

            @pl.when(inside(ahead(s, d)))
            def _(d=d):
                total_out(s, d).start()

    def scan_back(s):
        base[...] = jnp.zeros_like(base)
        for d in by_distance(zs, 1):

            @pl.when(inside(behind(s, d)))
            def _(d=d):
                total_in(s, d).wait_recv()
                base[...] += got2[s, wrapped(behind(s, d))].astype(F32)

        for p in range(group):
            back[s, p] = (base[0:prow, :] + part[p, 0:prow, :]).astype(BF16)
        for copy in back_out(s):
            copy.start()
        got3[s, g] = back[s, g]
        all_sums[s] = base[prow : prow + PAD, :] + part[g, prow : prow + PAD, :]

    def scan_end(s):
        for copy in back_in(s):
            copy.wait_recv()

    def scan_memory(s, h):
        per = group // heads
        return jnp.concatenate([got3[s, h * per + j] for j in range(per)], 0)

    def scan_sums(s, h):
        return all_sums[s, h : h + 1, :]

    def scan_sent(s):
        for copy in slices_out(s):
            copy.wait_send()
        for d in by_distance(zs, 1):

            @pl.when(inside(ahead(s, d)))
            def _(d=d):
                total_out(s, d).wait_send()

        for copy in back_out(s):
            copy.wait_send()

    def cols(h):
        return pl.ds(h * HD, HD)

    def gate_of(h):
        return jax.nn.sigmoid(jnp.full((1, HD), beta[h], F32))

    blocks = length // BLOCK

    def attention(h):
        for i in range(blocks):
            q_rows, seen = pl.ds(i * BLOCK, BLOCK), pl.ds(0, (i + 1) * BLOCK)
            s_t = dot_nt(k_v[seen, cols(h)], q_v[q_rows, cols(h)]) * scale
            key_at = lax.broadcasted_iota(jnp.int32, s_t.shape, 0)
            query_at = lax.broadcasted_iota(jnp.int32, s_t.shape, 1) + i * BLOCK
            s_t = jnp.where(key_at <= query_at, s_t, -jnp.inf)
            e = jnp.exp(s_t - jnp.max(s_t, 0, keepdims=True))
            p = e * (1.0 / jnp.sum(e, 0, keepdims=True))
            probs[h, seen, q_rows] = p
            local_out[q_rows, cols(h)] = dot_tn(p.astype(BF16), v_v[seen, cols(h)])

    def attention_back(h):
        gate = gate_of(h)
        memory, sums = scan_memory(0, h), scan_sums(0, h)
        for i in reversed(range(blocks)):
            q_rows, seen = pl.ds(i * BLOCK, BLOCK), pl.ds(0, (i + 1) * BLOCK)
            g_f = gm[q_rows, cols(h)].astype(F32)
            g_l = ((1.0 - gate) * g_f).astype(BF16)
            q_b = q_v[q_rows, cols(h)]
            p = probs[h, seen, q_rows]
            gp = dot_nt(v_v[seen, cols(h)], g_l)
            delta = jnp.sum(p * gp, 0, keepdims=True)
            gs = (p * (gp - delta) * scale).astype(BF16)
            k_add, v_add = dot_nn(gs, q_b), dot_nn(p.astype(BF16), g_l)
            if i == blocks - 1:
                kl[seen, cols(h)] = k_add
                vl[seen, cols(h)] = v_add
            else:
                kl[seen, cols(h)] += k_add
                vl[seen, cols(h)] += v_add
            g_q = dot_nt(grad_n[q_rows, cols(h)], memory) + grad_d[h, q_rows, :] * sums
            own = dot_tn(gs, k_v[seen, cols(h)])
            gq_v[q_rows, cols(h)] = (own + g_q * q_slope[q_rows, cols(h)]).astype(BF16)

    loads[0].wait()
    loads[1].wait()
    memories, sums = [], []
    for h in range(heads):
        if h == 2:
            pl.semaphore_wait(barrier, len(peers))
            for i in range(4):
                cot_out[i].start()
        kf, k_slope[:, cols(h)] = feat_slope(k_v[:, cols(h)].astype(F32))
        kf_h = kf.astype(BF16)
        kf_b[:, cols(h)] = kf_h
        memories.append(dot_tn(kf_h, v_v[:, cols(h)]))
        sums.append(jnp.sum(kf, 0, keepdims=True))
    scan_put(0, memories, sums)
    scan_start(0)
    loads[2].wait()
    for h in range(heads):
        attention(h)
    scan_middle(0)
    cot_relay()

    def block_rows(b):
        return pl.ds(pl.multiple_of(b * rows, rows), rows)

    def grad_in(b):
        gm[block_rows(b), :] = dot_nt(cot_v[b], w_v[...]).astype(BF16)

    def project(b, slot):
        pf[slot] = dot_nn(mixed[block_rows(b), :], w_v[...])

    def rs_copy(i, to):
        return remote(rs_src.at[i], rs_dst.at[i], rs_send.at[i], rs_recv.at[i], to)

    rs = [rs_copy(i, to_right if i % 2 == 0 else to_left) for i in range(6)]

    def rs_start(i, piece):
        rs_src[i] = piece.astype(BF16)
        rs[i].start()

    loads[3].wait()
    loads[4].wait()
    grad_in(y)
    for h in range(heads):
        q_feat[:, cols(h)], q_slope[:, cols(h)] = feat_slope(q_v[:, cols(h)].astype(F32))
    scan_back(0)

    for h in range(heads):
        near = jnp.sum(q_feat[:, cols(h)] * scan_sums(0, h), -1, keepdims=True)
        rdenom[h] = 1.0 / (near + 1.0)

    def grad_block(b, start):
        part_rows = block_rows(b)
        for h in range(heads):
            g_m = gate_of(h) * gm[part_rows, cols(h)].astype(F32)
            g_n = (g_m * rdenom[h, part_rows, :]).astype(BF16)
            grad_n[part_rows, cols(h)] = g_n
            memory = dot_tn(q_feat[part_rows, cols(h)].astype(BF16), g_n)
            grad_mem[h] = memory if start else grad_mem[h] + memory

    def grad_row(b, start):
        part_rows = block_rows(b)
        for h in range(heads):
            g_m = gate_of(h) * gm[part_rows, cols(h)].astype(F32)
            over = jnp.sum(g_m * mem_out[part_rows, cols(h)], -1, keepdims=True)
            g_d = -over * rdenom[h, part_rows, :]
            grad_d[h, part_rows, :] = g_d
            total_d = jnp.sum(g_d * q_feat[part_rows, cols(h)], 0, keepdims=True)
            grad_sum[h] = total_d if start else grad_sum[h] + total_d

    grad_block(y, True)
    cot_arrive[2].wait_recv()
    grad_in(left)
    grad_block(left, False)
    cot_arrive[3].wait_recv()
    grad_in(right)
    grad_block(right, False)
    scan_end(0)

    def read_block(b):
        part_rows = block_rows(b)
        for h in range(heads):
            gate = gate_of(h)
            q_b = q_feat[part_rows, cols(h)].astype(BF16)
            m_o = dot_nn(q_b, scan_memory(0, h)) * rdenom[h, part_rows, :]
            mem_out[part_rows, cols(h)] = m_o
            mix = gate * m_o + (1.0 - gate) * local_out[part_rows, cols(h)]
            mixed[part_rows, cols(h)] = mix.astype(BF16)

    read_block(far)
    project(far, 0)
    rs_start(0, pf[0, 0:half, :])
    rs_start(1, pf[0, half:rows, :])
    read_block(right)
    read_block(left)
    read_block(y)
    grad_row(y, True)
    grad_row(left, False)
    grad_row(right, False)
    cot_arrive[4].wait_recv()
    cot_arrive[5].wait_recv()
    grad_in(far)
    grad_block(far, False)
    grad_row(far, False)
    scan_put(1, [grad_mem[h] for h in range(heads)], [grad_sum[h] for h in range(heads)])
    scan_start(1)
    project(right, 1)
    rs_start(2, pf[1, half:rows, :])
    project(left, 2)
    rs_start(3, pf[2, 0:half, :])
    attention_back(0)
    scan_middle(1)
    attention_back(1)
    attention_back(2)
    rs[0].wait_recv()
    rs_start(4, pf[1, 0:half, :] + rs_dst[0].astype(F32))
    rs[1].wait_recv()
    rs_start(5, pf[2, half:rows, :] + rs_dst[1].astype(F32))
    scan_back(1)
    attention_back(3)
    project(y, 3)
    for i in range(2, 6):
        rs[i].wait_recv()
    out_v[0:half, :] = (
        pf[3, 0:half, :] + rs_dst[4].astype(F32) + rs_dst[3].astype(F32)
    ).astype(BF16)
    out_v[half:rows, :] = (
        pf[3, half:rows, :] + rs_dst[2].astype(F32) + rs_dst[5].astype(F32)
    ).astype(BF16)

    scan_end(1)
    for h in range(heads):
        memory, sums = scan_memory(1, h), scan_sums(1, h)
        g_k = dot_nt(v_v[:, cols(h)], memory) + sums
        gk_v[:, cols(h)] = (kl[:, cols(h)] + g_k * k_slope[:, cols(h)]).astype(BF16)
        gv_v[:, cols(h)] = (vl[:, cols(h)] + dot_nn(kf_b[:, cols(h)], memory)).astype(BF16)

    for copy in cot_out:
        copy.wait_send()
    for copy in rs:
        copy.wait_send()
    scan_sent(0)
    scan_sent(1)


def store(*refs):
    sources, targets, sem = refs[:4], refs[4:8], refs[8]
    copies = [
        pltpu.make_async_copy(src, dst, sem.at[i])
        for i, (src, dst) in enumerate(zip(sources, targets))
    ]
    for copy in copies:
        copy.start()
    for copy in copies:
        copy.wait()


def solution(mesh):
    split = Mesh(mesh.devices.reshape(8, 4, 2, mesh.shape["tp"]), SEQ_TP)
    zs, xs, cs, ts = split.devices.shape
    group = xs * cs

    def local(query, keys, values, beta, out_weight, cotangent):
        length, width = query.shape
        heads = width // HD
        rows, deep = cotangent.shape
        prow = heads * HD // group
        slab = prow + PAD
        vm = pltpu.VMEM
        dma = pltpu.SemaphoreType.DMA
        any_ = pl.BlockSpec(memory_space=pl.ANY)
        scratch = [
            vm((length, width), BF16), vm((length, width), BF16), vm((length, width), BF16),
            vm((width, deep), BF16), vm((ts, rows, deep), BF16), dma((5,)),
            dma((6,)), dma((6,)),
            vm((2, group, slab, HD), BF16), vm((2, group, slab, HD), BF16),
            vm((group, slab, HD), F32), vm((2, slab, HD), BF16), vm((slab, HD), F32),
            vm((2, zs, slab, HD), BF16),
            vm((2, group, prow, HD), BF16), vm((2, group, prow, HD), BF16), vm((2, PAD, HD), F32),
            dma((2, 3, 8)), dma((2, 3, 8)),
            vm((heads, length, length), F32), vm((length, width), F32), vm((length, width), F32),
            vm((heads, length, 1), F32), vm((length, width), BF16), vm((length, width), BF16),
            vm((length, width), F32), vm((length, width), F32),
            vm((length, width), BF16), vm((length, width), F32), vm((length, width), F32),
            vm((length, width), F32), vm((length, width), BF16), vm((heads, length, 1), F32),
            vm((heads, HD, HD), F32), vm((heads, 1, HD), F32),
            vm((ts, rows, deep), F32), vm((6, rows // 2, deep), BF16), vm((6, rows // 2, deep), BF16),
            dma((6,)), dma((6,)),
        ]
        results = ((rows, deep), (length, width), (length, width), (length, width))
        held = pl.pallas_call(
            functools.partial(kernel, zs, xs, cs, ts),
            out_shape=tuple(vm(dims, BF16) for dims in results),
            in_specs=[any_, any_, any_, pl.BlockSpec(memory_space=pltpu.SMEM), any_, any_],
            out_specs=(pl.BlockSpec(memory_space=pltpu.VMEM),) * 4,
            scratch_shapes=scratch,
            compiler_params=pltpu.CompilerParams(
                collective_id=0, has_side_effects=True, vmem_limit_bytes=58 * 1024 * 1024
            ),
            cost_estimate=pl.CostEstimate(
                flops=5_000_000_000, bytes_accessed=8_000_000, transcendentals=2_000_000
            ),
            name="layer",
        )(query, keys, values, beta, out_weight, cotangent)
        return pl.pallas_call(
            store,
            out_shape=tuple(jax.ShapeDtypeStruct(dims, BF16) for dims in results),
            in_specs=[any_] * 4,
            out_specs=(any_,) * 4,
            scratch_shapes=[dma((4,))],
            compiler_params=pltpu.CompilerParams(vmem_limit_bytes=4 * 1024 * 1024),
            cost_estimate=pl.CostEstimate(flops=0, bytes_accessed=4_000_000, transcendentals=0),
            name="store",
        )(*held)

    placed = (P(SEQ, "tp"), P(SEQ, "tp"), P(SEQ, "tp"), P("tp"), P("tp", None), P(SEQ_TP, None))
    return jax.shard_map(
        local,
        mesh=split,
        in_specs=placed,
        out_specs=(P(SEQ_TP, None), P(SEQ, "tp"), P(SEQ, "tp"), P(SEQ, "tp")),
        check_vma=False,
    )
```
